32 devices in a mesh: dp: 16 (over z, y, core), seq: 2 (over x).
Axes of the slice: x: 2, y: 2, z: 4, core: 2. Of those that a mesh axis runs over, the one named last changes fastest.
Arguments:
- tokens: bfloat16 [256, 200, 512], P(('dp', 'seq')), may hold values from -6 to 6
- w_qkv: bfloat16 [512, 1536], P(('dp', 'seq')), may hold values from -0.25 to 0.25
- w_attn_out: bfloat16 [512, 512], P(('dp', 'seq')), may hold values from -2 to 2
- w_router: bfloat16 [512, 16], P(('dp', 'seq')), may hold values from -0.1875 to 0.1875
- gain_attn: bfloat16 [512], P(('dp', 'seq')), may hold values from 0.5 to 1.5
- gain_moe: bfloat16 [512], P(('dp', 'seq')), may hold values from 0.5 to 1.5
- w_expert_in: bfloat16 [16, 512, 2048], P('dp', 'seq'), may hold values from -0.25 to 0.25
- w_expert_down: bfloat16 [16, 512, 2048], P('dp', 'seq'), may hold values from -4 to 4
- key_mask: int32 [256, 200], P('dp'), may hold values from 0 to 1, as said below
- expert_choice: int32 [256, 200, 2], P(('dp', 'seq')), may hold values from 0 to 15, as said below
- slot_index: int32 [256, 200, 2], P(('dp', 'seq')), may hold values from -1 to 255, as said below
- cotangent: bfloat16 [256, 200, 512], P(('dp', 'seq')), may hold values from -6 to 6
Outputs:
- mixed_out: bfloat16 [256, 200, 512], P(('dp', 'seq'))
- grad_tokens: float32 [256, 200, 512], P(('dp', 'seq'))
- grad_w_qkv: float32 [512, 1536], P(('dp', 'seq'))
- grad_w_attn_out: float32 [512, 512], P(('dp', 'seq'))
- grad_w_router: float32 [512, 16], P(('dp', 'seq'))
- grad_gain_attn: float32 [512], P(('dp', 'seq'))
- grad_gain_moe: float32 [512], P(('dp', 'seq'))
- grad_w_expert_in: float32 [16, 512, 2048], P('dp', 'seq')
- grad_w_expert_down: float32 [16, 512, 2048], P('dp', 'seq')
The draws below stay inside these ranges and needn't reach their ends.
Inputs may be any that keep to these rules, and one draw needn't show every extreme that they name: `key_mask`: each image's row is a run of ones from position 0 followed by zeros, with 150 ones or more; in each group of 16 images of one index of dp some image has no padding. `expert_choice`: the two choices of a token differ. `slot_index`: among the tokens of one device (its 8 images), the kept choices that name one expert have distinct slots; a choice is -1 when it is dropped.
All inputs are finite; a program needn't handle non-finite values.
Results may differ from the reference program's by a relative error of at most 0.017.
Values may be sent and summed in bfloat16 or wider, within the bound.
A program may use at most 256 MiB of HBM per device.

```python
import jax
import jax.numpy as jnp
from jax import lax

D = 512
HEADS = 8
HEAD_DIM = 64
FFH = 2048
TOPK = 2
LPAD = 200
IMG_U = 8
IMG_DP = 16
IMAGES = 256
EXPERTS = 16
CAP = 256
N_DP = 16
N_SEQ = 2


def route_table(key):
    key_first, key_offset, key_plant = jax.random.split(key, 3)
    blocks = IMAGES // IMG_U
    per_block = IMG_U * LPAD
    first_pick = jax.random.randint(key_first, (blocks, per_block), 0, EXPERTS)
    offset_pick = jax.random.randint(key_offset, (blocks, per_block), 1, EXPERTS)
    planted = jax.random.randint(key_plant, (blocks, 1), 0, EXPERTS)
    first_pick = jnp.where(jnp.arange(per_block)[None, :] < CAP, planted, first_pick)
    second_pick = (first_pick + offset_pick) % EXPERTS
    chosen = jnp.stack([first_pick, second_pick], axis=-1).reshape(blocks, per_block * TOPK)
    hits = (chosen[..., None] == jnp.arange(EXPERTS)[None, None, :]).astype(jnp.int32)
    ranks = jnp.cumsum(hits, axis=1) - 1
    slots = jnp.sum(ranks * hits, axis=-1)
    slots = jnp.where(slots < CAP, slots, -1)
    return (chosen.reshape(IMAGES, LPAD, TOPK).astype(jnp.int32), slots.reshape(IMAGES, LPAD, TOPK).astype(jnp.int32))


def draw_expert_choice(key, part):
    chosen_table, slot_table = route_table(key)
    return chosen_table


def draw_slot_index(key, part):
    chosen_table, slot_table = route_table(key)
    return slot_table


def draw_key_mask(key, part):
    key = jax.random.fold_in(key, 11)
    key_length, key_full = jax.random.split(key)
    lengths = jax.random.randint(key_length, (IMAGES,), LPAD * 3 // 4, LPAD + 1)
    full_pick = jax.random.randint(key_full, (IMAGES // IMG_DP,), 0, IMG_DP)
    is_full = jnp.arange(IMAGES) % IMG_DP == jnp.repeat(full_pick, IMG_DP)
    lengths = jnp.where(is_full, LPAD, lengths)
    return (jnp.arange(LPAD)[None, :] < lengths[:, None]).astype(jnp.int32)


def steps_of(key, shape, cuts, smallest, high):
    gain = 1.0
    for dim, blocks in cuts:
        steps = jax.random.uniform(jax.random.fold_in(jax.random.fold_in(key, 6), dim), (blocks,), jnp.float32, smallest / len(cuts), high / len(cuts))
        gain = gain * jnp.repeat(jnp.exp(steps), shape[dim] // blocks).reshape((-1,) + (1,) * (len(shape) - 1 - dim))
    return gain


def bell_draw(own_key, dims, deviation, most, cuts=(), held_as=jnp.bfloat16):
    gain = steps_of(own_key, dims, cuts, -0.22, 0.18) if cuts else 1.0
    array = jax.random.normal(own_key, dims, jnp.float32) * deviation * gain
    return jnp.minimum(jnp.maximum(array, -most), most).astype(held_as)


def setup_inputs(seed: int = 0) -> dict:
    key_of = jax.random.split(jax.random.key(seed), 13)
    tokens = bell_draw(key_of[0], (IMAGES, LPAD, D), 1.0, 6.0, ((0, 32),))
    w_qkv = bell_draw(key_of[1], (D, 3 * D), D ** -0.5, 0.25, ((0, 32),))
    w_attn_out = bell_draw(key_of[2], (D, D), (D // 64) ** -0.5, 2.0, ((0, 32),))
    w_router = bell_draw(key_of[3], (D, EXPERTS), (2 * D) ** -0.5, 0.1875, ((0, 32),))
    gain_attn = jnp.clip(1.0 + 0.1 * jax.random.normal(key_of[4], (D,), jnp.float32), 0.5, 1.5).astype(jnp.bfloat16)
    gain_moe = jnp.clip(1.0 + 0.1 * jax.random.normal(key_of[5], (D,), jnp.float32), 0.5, 1.5).astype(jnp.bfloat16)
    w_expert_in = bell_draw(key_of[6], (EXPERTS, D, FFH), D ** -0.5, 0.25, ((0, 16), (1, 2)))
    w_expert_down = bell_draw(key_of[7], (EXPERTS, D, FFH), (max(FFH // 1024, 1)) ** -0.5, 4.0, ((0, 16), (1, 2)))
    key_mask = draw_key_mask(jax.random.fold_in(key_of[12], 71), 0)
    expert_choice = draw_expert_choice(jax.random.fold_in(key_of[12], 71), 0)
    slot_index = draw_slot_index(jax.random.fold_in(key_of[12], 71), 0)
    cotangent = bell_draw(key_of[11], (IMAGES, LPAD, D), 1.0, 6.0, ((0, 32),))
    return {"tokens": tokens, "w_qkv": w_qkv, "w_attn_out": w_attn_out, "w_router": w_router, "gain_attn": gain_attn, "gain_moe": gain_moe, "w_expert_in": w_expert_in, "w_expert_down": w_expert_down, "key_mask": key_mask, "expert_choice": expert_choice, "slot_index": slot_index, "cotangent": cotangent}


EPSILON = 1e-06
NEGATIVE = -1e+30
HIGHEST = lax.Precision.HIGHEST

@jax.custom_vjp
def low(v):
    return lax.optimization_barrier(v.astype(jnp.bfloat16)).astype(jnp.float32)

@jax.custom_vjp
def low_back(v):
    return v

def low_keep(v):
    return (low(v), None)

def low_pass(kept, grad):
    return (grad,)

def back_keep(v):
    return (v, None)

def back_low(kept, grad):
    return (low(grad),)
low.defvjp(low_keep, low_pass)
low_back.defvjp(back_keep, back_low)

def layer_norm(values, gain_vec):
    centred = values - lax.optimization_barrier(jnp.mean(values, axis=-1, keepdims=True))
    return centred * lax.rsqrt(lax.optimization_barrier(jnp.mean(centred * centred, axis=-1, keepdims=True)) + EPSILON) * gain_vec

def reference(tokens, w_qkv, w_attn_out, w_router, gain_attn, gain_moe, w_expert_in, w_expert_down, key_mask, expert_choice, slot_index, cotangent):
    key_keep = key_mask > 0
    image_ids = jnp.arange(IMAGES, dtype=jnp.int32)[:, None]
    block_ids = jnp.broadcast_to(image_ids // IMG_U, (IMAGES, LPAD)).astype(jnp.int32)
    expert_rows = N_DP * N_SEQ * CAP
    target = jnp.where(slot_index >= 0, expert_choice * expert_rows + block_ids[:, :, None] * CAP + slot_index, EXPERTS * expert_rows).astype(jnp.int32)
    onehot_pick = (expert_choice[..., None] == jnp.arange(EXPERTS, dtype=jnp.int32)).astype(jnp.float32)
    groups = IMAGES // IMG_U
    score_scale = HEAD_DIM ** (-0.5)

    def attend(image_block):
        queries, keys_in, values_in, keep_block = image_block
        scores = low_back(jnp.einsum('iqhd,ikhd->ihqk', queries, keys_in, precision=HIGHEST) * score_scale)
        scores = jnp.where(keep_block[:, None, None, :], scores, NEGATIVE)
        weights = low(jax.nn.softmax(scores, axis=-1))
        return jnp.einsum('ihqk,ikhd->iqhd', weights, values_in, precision=HIGHEST)

    def expert(expert_item):
        rows_in, weight_in, weight_down = expert_item
        inner_rows = low_back(jnp.dot(rows_in, weight_in, precision=HIGHEST))
        activated = low(jax.nn.gelu(inner_rows))
        return low_back(low(jnp.dot(activated, weight_down.T, precision=HIGHEST)))

    def forward(inputs, weight_qkv, weight_out, weight_router, gain_one, gain_two, weight_in, weight_down):
        normed = low(layer_norm(inputs, gain_one))
        projected = low_back(low(jnp.einsum('ild,de->ile', normed, weight_qkv, precision=HIGHEST)))

        def head_part(offset):
            return projected[..., offset * D:(offset + 1) * D].reshape(groups, IMG_U, LPAD, HEADS, HEAD_DIM)
        attended = lax.map(jax.checkpoint(attend), (head_part(0), head_part(1), head_part(2), key_keep.reshape(groups, IMG_U, LPAD)))
        attended = low_back(low(attended.reshape(IMAGES, LPAD, D)))
        residual = inputs + low_back(jnp.einsum('ild,de->ile', attended, weight_out, precision=HIGHEST))
        routed = low(layer_norm(residual, gain_two))
        router_probs = jax.nn.softmax(jnp.einsum('ild,de->ile', routed, weight_router, precision=HIGHEST), axis=-1)
        gate_values = lax.optimization_barrier(jnp.sum(onehot_pick * router_probs[:, :, None, :], axis=-1))
        pair_rows = jnp.broadcast_to(routed[:, :, None, :], (IMAGES, LPAD, TOPK, D)).reshape(IMAGES * LPAD * TOPK, D)
        buffer_rows = jnp.zeros((EXPERTS * expert_rows, D), routed.dtype).at[target.reshape(-1)].set(pair_rows, mode='drop')
        dispatched = low_back(buffer_rows).reshape(EXPERTS, expert_rows, D)
        outputs = lax.map(jax.checkpoint(expert), (dispatched, weight_in, weight_down))
        paired = jnp.take(outputs.reshape(EXPERTS * expert_rows, D), target, axis=0, mode='fill', fill_value=0.0)
        return residual + lax.optimization_barrier(jnp.sum(gate_values[..., None] * paired, axis=2))
    primal = (tokens.astype(jnp.float32), w_qkv.astype(jnp.float32), w_attn_out.astype(jnp.float32), w_router.astype(jnp.float32), gain_attn.astype(jnp.float32), gain_moe.astype(jnp.float32), w_expert_in.astype(jnp.float32), w_expert_down.astype(jnp.float32))
    mixed, pull_back = jax.vjp(forward, *primal)
    gradients = pull_back(cotangent.astype(jnp.float32))
    return (mixed.astype(jnp.bfloat16), gradients[0], gradients[1], gradients[2], gradients[3], gradients[4], gradients[5], gradients[6], gradients[7])
```

```python
import functools

import jax
import jax.numpy as jnp
from jax import lax
from jax.experimental import pallas as pl
from jax.experimental.pallas import tpu as pltpu
from jax.sharding import PartitionSpec as P

HEADS = 8
EPSILON = 1e-06
NEGATIVE = -1e30
MESH = pl.DeviceIdType.MESH
bf16, f32 = jnp.bfloat16, jnp.float32
NN = (((1,), (0,)), ((), ()))
NT = (((1,), (1,)), ((), ()))
TN = (((0,), (0,)), ((), ()))
LANES = 128
GAIN_LANE = 64
VMEM_LIMIT = 60 << 20
Shape = jax.ShapeDtypeStruct


def dot(a, b, dims=NN):
    return lax.dot_general(a, b, dims, preferred_element_type=f32)


def pad_rows(values, rows):
    extra = rows - values.shape[0]
    if extra == 0:
        return values
    return jnp.concatenate([values, jnp.zeros((extra, values.shape[1]), values.dtype)], axis=0)


def norm_rows(values):
    centred = values - jnp.mean(values, axis=-1, keepdims=True)
    inverse = lax.rsqrt(jnp.mean(centred * centred, axis=-1, keepdims=True) + EPSILON)
    return centred * inverse, inverse


def norm_back(grad_hat, normed, inverse):
    return inverse * (
        grad_hat
        - jnp.mean(grad_hat, axis=-1, keepdims=True)
        - normed * jnp.mean(grad_hat * normed, axis=-1, keepdims=True)
    )


def router_softmax(logits, experts):
    lane = lax.broadcasted_iota(jnp.int32, logits.shape, 1)
    logits = jnp.where(lane < experts, logits, NEGATIVE)
    exps = jnp.exp(logits - jnp.max(logits, axis=1, keepdims=True))
    return exps / jnp.sum(exps, axis=1, keepdims=True)


def gelu_parts(inner):
    k, c = 0.7978845608028654, 0.044715
    square = inner * inner
    t = jnp.tanh(inner * (k + (k * c) * square))
    half = 0.5 + 0.5 * t
    value = inner * half
    slope = half + value * (1.0 - half) * (2 * k + (6 * k * c) * square)
    return value, slope


def vmem():
    return pl.BlockSpec(memory_space=pltpu.VMEM)


def anywhere():
    return pl.BlockSpec(memory_space=pl.ANY)


def per_image(*dims):
    return pl.BlockSpec((1,) + dims, lambda i: (i,) + (0,) * len(dims))


def fixed(*dims):
    return pl.BlockSpec(dims, lambda i: (0,) * len(dims))


class Layout:
    def __init__(self, dp, seq):
        self.N, self.S = dp, seq
        self.L = dp // seq

    def here(self):
        dp, s = lax.axis_index("dp"), lax.axis_index("seq")
        return dp, s, dp // self.L, lax.rem(dp, self.L)

    def member_device(self, g, m):
        return (g * self.L + m // self.S, lax.rem(m, self.S))

    def expert_of(self, g, m):
        l, s = m // self.S, lax.rem(m, self.S)
        return lax.rem(g + s + l, self.S) * self.L + l


def greet(peers):
    barrier = pltpu.get_barrier_semaphore()
    for peer in peers:
        pl.semaphore_signal(barrier, inc=1, device_id=peer, device_id_type=MESH)
    pl.semaphore_wait(barrier, len(peers))


class Rows:
    def __init__(self, dp, seq):
        self.A, self.S = dp // 4, seq

    def here(self):
        dp, s = lax.axis_index("dp"), lax.axis_index("seq")
        return dp // 4, lax.rem(dp // 2, 2), lax.rem(dp, 2), s

    def device(self, a, b, c, s):
        return ((a * 2 + b) * 2 + c, s)

    def along_a(self):
        a, b, c, s = self.here()
        return [(i, lax.rem(a + i, self.A)) for i in range(1, self.A)]

    def plane(self):
        a, b, c, s = self.here()
        for i in range(1, 2 * self.S):
            if self.S == 1:
                yield i, 1 - b, s, 0
            else:
                q = lax.rem(b * self.S + s + i, 2 * self.S)
                yield i, q // self.S, lax.rem(q, self.S), lax.rem(q, self.S)


def gather_kernel(rows, own_ref, full_ref, ssem, rsem, lsem):
    a, b, c, s = rows.here()
    sl = s if rows.S > 1 else 0
    greet(
        [rows.device(i, b, c, s) for _, i in rows.along_a()]
        + [rows.device(a, b2, c, s2) for _, b2, s2, _ in rows.plane()]
        + [rows.device(a, b, 1 - c, s)]
    )
    A, Q = rows.A, 2 * rows.S
    own = pltpu.make_async_copy(own_ref, full_ref.at[a, b, c, sl], lsem)
    own.start()
    copies = []
    for i, a2 in rows.along_a():
        copies.append(
            pltpu.make_async_remote_copy(
                own_ref, full_ref.at[a, b, c, sl], ssem.at[i], rsem.at[i],
                device_id=rows.device(a2, b, c, s), device_id_type=MESH,
            )
        )
        copies[-1].start()
    own.wait()
    for copy in copies:
        copy.wait()
    copies = []
    for i, b2, s2, _ in rows.plane():
        copies.append(
            pltpu.make_async_remote_copy(
                full_ref.at[:, b, c, sl], full_ref.at[:, b, c, sl], ssem.at[A + i], rsem.at[A + i],
                device_id=rows.device(a, b2, c, s2), device_id_type=MESH,
            )
        )
        copies[-1].start()
    for copy in copies:
        copy.wait()
    last = pltpu.make_async_remote_copy(
        full_ref.at[:, :, c], full_ref.at[:, :, c], ssem.at[A + Q], rsem.at[A + Q],
        device_id=rows.device(a, b, 1 - c, s), device_id_type=MESH,
    )
    last.start()
    last.wait()


def gather_rows(rows, own):
    height, width = own.shape
    count = rows.A + 2 * rows.S + 1
    full = pl.pallas_call(
        functools.partial(gather_kernel, rows),
        out_shape=Shape((rows.A, 2, 2, rows.S, height, width), own.dtype),
        in_specs=[vmem()],
        out_specs=vmem(),
        scratch_shapes=[
            pltpu.SemaphoreType.DMA((count,)),
            pltpu.SemaphoreType.DMA((count,)),
            pltpu.SemaphoreType.DMA,
        ],
        compiler_params=pltpu.CompilerParams(collective_id=0, has_side_effects=True, vmem_limit_bytes=VMEM_LIMIT),
    )(own)
    return full.reshape(rows.A * 4 * rows.S * height, width)


def scatter_kernel(rows, qkv_ref, out_ref, rest_ref, own_ref, part, recv1, sum1, recv2, sum2, recv3, ssem, rsem):
    a, b, c, s = rows.here()
    greet(
        [rows.device(i, b, c, s) for _, i in rows.along_a()]
        + [rows.device(a, b2, c, s2) for _, b2, s2, _ in rows.plane()]
        + [rows.device(a, b, 1 - c, s)]
    )
    A, S, Q = rows.A, rows.S, 2 * rows.S
    height = part.shape[4]
    wq, wo = qkv_ref.shape[1], out_ref.shape[1]
    for i in range(A * 4 * S):
        where = (i // (4 * S), (i // (2 * S)) % 2, (i // S) % 2, i % S)
        span = slice(i * height, (i + 1) * height)
        part[where + (slice(None), slice(0, wq))] = qkv_ref[span, :].astype(bf16)
        part[where + (slice(None), slice(wq, wq + wo))] = out_ref[span, :].astype(bf16)
        part[where + (slice(None), slice(wq + wo, None))] = rest_ref[span, :].astype(bf16)
    first = pltpu.make_async_remote_copy(
        part.at[:, :, 1 - c], recv1, ssem.at[0], rsem.at[0],
        device_id=rows.device(a, b, 1 - c, s), device_id_type=MESH,
    )
    first.start()
    first.wait()
    sum1[...] = (part[:, :, c].astype(f32) + recv1[...].astype(f32)).astype(bf16)
    copies = []
    for i, b2, s2, sl2 in rows.plane():
        copies.append(
            pltpu.make_async_remote_copy(
                sum1.at[:, b2, sl2], recv2.at[i - 1], ssem.at[i], rsem.at[i],
                device_id=rows.device(a, b2, c, s2), device_id_type=MESH,
            )
        )
        copies[-1].start()
    for copy in copies:
        copy.wait()
    sl = s if S > 1 else 0
    total = sum1[:, b, sl].astype(f32)
    for i in range(Q - 1):
        total += recv2[i].astype(f32)
    sum2[...] = total.astype(bf16)
    copies = []
    for i, a2 in rows.along_a():
        copies.append(
            pltpu.make_async_remote_copy(
                sum2.at[a2], recv3.at[i - 1], ssem.at[Q + i], rsem.at[Q + i],
                device_id=rows.device(a2, b, c, s), device_id_type=MESH,
            )
        )
        copies[-1].start()
    for copy in copies:
        copy.wait()
    final = sum2[a].astype(f32)
    for i in range(A - 1):
        final += recv3[i].astype(f32)
    own_ref[...] = final


def scatter_rows(rows, grad_qkv, grad_out, grad_rest):
    A, S = rows.A, rows.S
    width = grad_qkv.shape[1] + grad_out.shape[1] + grad_rest.shape[1]
    height = grad_qkv.shape[0] // (A * 4 * S)
    count = A + 2 * S + 1
    return pl.pallas_call(
        functools.partial(scatter_kernel, rows),
        out_shape=Shape((height, width), f32),
        in_specs=[vmem()] * 3,
        out_specs=vmem(),
        scratch_shapes=[
            pltpu.VMEM((A, 2, 2, S, height, width), bf16),
            pltpu.VMEM((A, 2, S, height, width), bf16),
            pltpu.VMEM((A, 2, S, height, width), bf16),
            pltpu.VMEM((2 * S - 1, A, height, width), bf16),
            pltpu.VMEM((A, height, width), bf16),
            pltpu.VMEM((A - 1, height, width), bf16),
            pltpu.SemaphoreType.DMA((count,)),
            pltpu.SemaphoreType.DMA((count,)),
        ],
        compiler_params=pltpu.CompilerParams(collective_id=2, has_side_effects=True, vmem_limit_bytes=VMEM_LIMIT),
    )(grad_qkv, grad_out, grad_rest)


def attend(heads, qkv, keep, width):
    head = width // heads
    outs, lses = [], []
    for h in range(heads):
        q = qkv[:, h * head : (h + 1) * head]
        k = qkv[:, width + h * head : width + (h + 1) * head]
        v = qkv[:, 2 * width + h * head : 2 * width + (h + 1) * head]
        scores = jnp.where(keep, dot(q, k, NT) * (head**-0.5), NEGATIVE)
        row_max = jnp.max(scores, axis=1, keepdims=True)
        exps = jnp.exp(scores - row_max)
        totals = jnp.sum(exps, axis=1, keepdims=True)
        lses.append(row_max + jnp.log(totals))
        outs.append(dot((exps / totals).astype(bf16), v).astype(bf16))
    return jnp.concatenate(outs, axis=1), jnp.concatenate(lses, axis=1)


def forward_kernel(
    experts, tok_ref, mask_ref, pack_ref, gains_ref, qkv_ref, att_ref, res_ref, lse_ref, routed_ref, probs_ref
):
    width = tok_ref.shape[2]
    rows = qkv_ref.shape[1]
    inputs = pad_rows(tok_ref[0].astype(f32), rows)
    hat, _ = norm_rows(inputs)
    normed = (hat * gains_ref[0:1, :]).astype(bf16)
    qkv = dot(normed, pack_ref[:, 0 : 3 * width]).astype(bf16)
    qkv_ref[0] = qkv
    att, lse = attend(HEADS, qkv, mask_ref[0] > 0, width)
    att_ref[0] = att
    lse_ref[0] = lse
    residual = inputs + dot(att, pack_ref[:, 3 * width : 4 * width])
    res_ref[0] = residual
    hat, _ = norm_rows(residual)
    routed = (hat * gains_ref[1:2, :]).astype(bf16)
    routed_ref[0] = routed
    probs_ref[0] = router_softmax(dot(routed, pack_ref[:, 4 * width :]), experts)


def forward(experts, rows, tokens, mask, pack, gains):
    images, positions, width = tokens.shape
    return pl.pallas_call(
        functools.partial(forward_kernel, experts),
        grid=(images,),
        out_shape=(
            Shape((images, rows, 3 * width), bf16),
            Shape((images, rows, width), bf16),
            Shape((images, rows, width), f32),
            Shape((images, rows, HEADS), f32),
            Shape((images, rows, width), bf16),
            Shape((images, rows, LANES), f32),
        ),
        in_specs=[per_image(positions, width), per_image(1, rows), vmem(), vmem()],
        out_specs=(
            per_image(rows, 3 * width),
            per_image(rows, width),
            per_image(rows, width),
            per_image(rows, HEADS),
            per_image(rows, width),
            per_image(rows, LANES),
        ),
        compiler_params=pltpu.CompilerParams(vmem_limit_bytes=VMEM_LIMIT),
        cost_estimate=pl.CostEstimate(flops=5 * 10**9, bytes_accessed=20 * 10**6, transcendentals=3 * 10**6),
    )(tokens, mask, pack, gains)


def expert_kernel(
    lay, experts, routed_ref, cot_ref, code_ref, router_ref, *refs
):
    S = lay.S
    w_refs, refs = refs[: 2 * S], refs[2 * S :]
    gx_ref, zy_ref, gate_ref, gwi_ref, gwd_ref = refs[:5]
    (w_in, w_down, cot, x_send, c_send, x_recv, c_recv, gx_send, zy_send, gate_send, gwi, gwd,
     wsem, xs, xr, cs, cr, gs, gr, zs, zr, ts, tr, lsem) = refs[5:]
    dp, s, g, l = lay.here()
    members, cap, width = x_send.shape
    me = l * S + s
    delta = lax.rem(s + l, S)
    slice_rows = w_in.shape[0] // S
    loads = []
    for j in range(S):
        first = pl.multiple_of(lax.rem(delta - j + S, S) * slice_rows, slice_rows)
        for which, target in ((0, w_in), (1, w_down)):
            loads.append(
                pltpu.make_async_copy(
                    w_refs[2 * j + which].at[0], target.at[pl.ds(first, slice_rows)], wsem.at[2 * j + which]
                )
            )
            loads[-1].start()
    greet([lay.member_device(g, jnp.bitwise_xor(me, k)) for k in range(1, members)])
    images, rows = routed_ref.shape[0], routed_ref.shape[1]
    for i in range(images):
        cot[i] = pad_rows(cot_ref[i].astype(f32), rows).astype(bf16)

    def remote(src, dst, send, recv, k):
        return pltpu.make_async_remote_copy(
            src, dst, send.at[k], recv.at[k],
            device_id=lay.member_device(g, jnp.bitwise_xor(me, k)), device_id_type=MESH,
        )

    def x_copy(k):
        return remote(x_send.at[jnp.bitwise_xor(me, k)], x_recv.at[me], xs, xr, k)

    def c_copy(k):
        return remote(c_send.at[jnp.bitwise_xor(me, k)], c_recv.at[me], cs, cr, k)

    def gx_copy(k):
        return remote(gx_send.at[jnp.bitwise_xor(me, k)], gx_ref.at[me], gs, gr, k)

    def zy_copy(k):
        return remote(zy_send.at[jnp.bitwise_xor(me, k)], zy_ref.at[me], zs, zr, k)

    def gate_copy(k):
        return remote(gate_send.at[jnp.bitwise_xor(me, k)], gate_ref.at[me], ts, tr, k)

    def dispatch(k, carry):
        m = jnp.bitwise_xor(me, k)
        slot = lax.broadcasted_iota(jnp.int32, (cap, images * rows), 0) + m * cap
        hit = (code_ref[0:1, :] == slot) | (code_ref[1:2, :] == slot)
        pick = jnp.where(hit, 1.0, 0.0).astype(bf16)
        x_send[m] = dot(pick, routed_ref[...].reshape(images * rows, width)).astype(bf16)
        c_send[m] = dot(pick, cot[...].reshape(images * rows, width)).astype(bf16)

        @pl.when(k > 0)
        def _():
            x_copy(k).start()
            c_copy(k).start()

        return carry

    lax.fori_loop(0, members, dispatch, 0)
    x_recv[me] = x_send[me]
    c_recv[me] = c_send[me]
    gwi[...] = jnp.zeros_like(gwi)
    gwd[...] = jnp.zeros_like(gwd)
    for load in loads:
        load.wait()
    mine = lay.expert_of(g, me)
    hidden = w_in.shape[1]
    chunk = min(512, hidden)

    def work(j, carry):
        ks = (2 * j, 2 * j + 1)
        ms = [jnp.bitwise_xor(me, k) for k in ks]

        @pl.when(j > 0)
        def _():
            x_copy(ks[0]).wait_recv()
            c_copy(ks[0]).wait_recv()

        x_copy(ks[1]).wait_recv()
        c_copy(ks[1]).wait_recv()
        x = jnp.concatenate([x_recv[m] for m in ms], axis=0)
        cf = jnp.concatenate([c_recv[m] for m in ms], axis=0).astype(f32)
        probs = router_softmax(dot(x, router_ref[...]), experts)
        lane = lax.broadcasted_iota(jnp.int32, probs.shape, 1)
        gate = jnp.sum(jnp.where(lane == mine, probs, 0.0), axis=1, keepdims=True)
        dy = (gate * cf).astype(bf16)
        y, gx = None, None
        for f in range(0, hidden, chunk):
            span = slice(f, f + chunk)
            value, slope = gelu_parts(dot(x, w_in[:, span]))
            act = value.astype(bf16)
            inner_grad = (dot(dy, w_down[:, span]) * slope).astype(bf16)
            y_part, gx_part = dot(act, w_down[:, span], NT), dot(inner_grad, w_in[:, span], NT)
            y = y_part if y is None else y + y_part
            gx = gx_part if gx is None else gx + gx_part
            gwd[:, span] += dot(dy, act, TN)
            gwi[:, span] += dot(x, inner_grad, TN)
        zy = (gate * y).astype(bf16)
        gxb = gx.astype(bf16)
        gate_grad = jnp.broadcast_to(jnp.sum(y * cf, axis=1, keepdims=True), (2 * cap, LANES)).T
        for q in range(2):
            gx_send[ms[q]] = gxb[q * cap : (q + 1) * cap]
            zy_send[ms[q]] = zy[q * cap : (q + 1) * cap]
            gate_send[ms[q]] = gate_grad[0:8, q * cap : (q + 1) * cap]

        @pl.when(j > 0)
        def _():
            gx_copy(ks[0]).start()
            gate_copy(ks[0]).start()
            zy_copy(ks[0]).start()

        gx_copy(ks[1]).start()
        gate_copy(ks[1]).start()
        zy_copy(ks[1]).start()
        return carry

    lax.fori_loop(0, members // 2, work, 0)
    keeps = [
        pltpu.make_async_copy(gx_send.at[me], gx_ref.at[me], lsem.at[0]),
        pltpu.make_async_copy(zy_send.at[me], zy_ref.at[me], lsem.at[1]),
        pltpu.make_async_copy(gate_send.at[me], gate_ref.at[me], lsem.at[2]),
    ]
    for keep in keeps:
        keep.start()
    for j in range(S):
        first = pl.multiple_of(lax.rem(delta - j + S, S) * slice_rows, slice_rows)
        gwi_ref[j] = gwi[pl.ds(first, slice_rows), :].astype(bf16)
        gwd_ref[j] = gwd[pl.ds(first, slice_rows), :].astype(bf16)
    for keep in keeps:
        keep.wait()

    def finish(k, carry):
        x_copy(k).wait_send()
        c_copy(k).wait_send()
        for copy in (gx_copy(k), zy_copy(k), gate_copy(k)):
            copy.wait()
        return carry

    lax.fori_loop(1, members, finish, 0)


def run_experts(lay, experts, cap, routed, cotangent, codes, router, weights):
    S, M = lay.S, lay.N
    images, rows, width = routed.shape
    hidden = weights[0].shape[-1]
    blocks = (M, cap, width)
    dma = pltpu.SemaphoreType.DMA((M,))
    return pl.pallas_call(
        functools.partial(expert_kernel, lay, experts),
        out_shape=(
            Shape(blocks, bf16),
            Shape(blocks, bf16),
            Shape((M, 8, cap), f32),
            Shape((S, width // S, hidden), bf16),
            Shape((S, width // S, hidden), bf16),
        ),
        in_specs=[vmem()] * 4 + [anywhere()] * (2 * S),
        out_specs=(anywhere(), anywhere(), vmem(), vmem(), vmem()),
        scratch_shapes=[
            pltpu.VMEM((width, hidden), bf16),
            pltpu.VMEM((width, hidden), bf16),
            pltpu.VMEM((images, rows, width), bf16),
            *[pltpu.VMEM(blocks, bf16)] * 6,
            pltpu.VMEM((M, 8, cap), f32),
            pltpu.VMEM((width, hidden), f32),
            pltpu.VMEM((width, hidden), f32),
            pltpu.SemaphoreType.DMA((2 * S,)),
            *[dma] * 10,
            pltpu.SemaphoreType.DMA((3,)),
        ],
        compiler_params=pltpu.CompilerParams(collective_id=1, has_side_effects=True, vmem_limit_bytes=VMEM_LIMIT),
    )(routed, cotangent, codes, router, *weights)


def backward_kernel(
    lay, tok_ref, mask_ref, cot_ref, code_ref, qkv_ref, att_ref, res_ref, lse_ref, routed_ref, probs_ref,
    pack_ref, gains_ref, gx_ref, gate_ref,
    gtok_ref, gqkv_ref, gout_ref, grest_ref, table, ggain,
):
    step = pl.program_id(0)
    _, _, g, _ = lay.here()
    images = pl.num_programs(0)
    members, _, cap = gate_ref.shape
    slots = members * cap
    rows, width = att_ref.shape[1], att_ref.shape[2]
    head = width // HEADS

    @pl.when(step == 0)
    def _():
        for ref in (gqkv_ref, gout_ref, grest_ref, ggain):
            ref[...] = jnp.zeros_like(ref)
        for m in range(members):
            values = gate_ref[m][0:1, :]
            high = values.astype(bf16).astype(f32)
            sub = lax.broadcasted_iota(jnp.int32, (LANES, cap), 0)
            here = sub == lay.expert_of(g, jnp.int32(m))
            span = slice(m * cap, (m + 1) * cap)
            table[0:LANES, span] = jnp.where(here, high, 0.0).astype(bf16)
            table[LANES : 2 * LANES, span] = jnp.where(here, values - high, 0.0).astype(bf16)

    code = code_ref[0]
    slot = lax.broadcasted_iota(jnp.int32, (rows, slots), 1)
    pick = jnp.where((code[:, 0:1] == slot) | (code[:, 1:2] == slot), 1.0, 0.0).astype(bf16)
    grad_routed = dot(pick, gx_ref[...].reshape(slots, width))
    both = dot(pick, table[...], NT)
    grad_probs = both[:, :LANES] + both[:, LANES:]
    probs = probs_ref[0]
    grad_logits = probs * (grad_probs - jnp.sum(grad_probs * probs, axis=1, keepdims=True))
    logit_high = grad_logits.astype(bf16)
    logit_low = (grad_logits - logit_high.astype(f32)).astype(bf16)
    router = pack_ref[:, 4 * width :]
    grad_router = dot(routed_ref[0], jnp.concatenate([logit_high, logit_low], axis=1), TN)
    grest_ref[...] += grad_router[:, :LANES] + grad_router[:, LANES:]
    grad_routed += dot(logit_high, router, NT) + dot(logit_low, router, NT)
    hat_two, inverse_two = norm_rows(res_ref[0])
    ggain[1:2, :] += jnp.sum(grad_routed * hat_two, axis=0, keepdims=True)
    grad_residual = pad_rows(cot_ref[0].astype(f32), rows) + norm_back(
        grad_routed * gains_ref[1:2, :], hat_two, inverse_two
    )
    grad_att = grad_residual.astype(bf16)
    gout_ref[...] += dot(att_ref[0], grad_att, TN)
    grad_attended = dot(grad_att, pack_ref[:, 3 * width : 4 * width], NT).astype(bf16)
    keep = mask_ref[0] > 0
    qkv, lse = qkv_ref[0], lse_ref[0]
    scale = head**-0.5
    grad_q, grad_k, grad_v = [], [], []
    for h in range(HEADS):
        q = qkv[:, h * head : (h + 1) * head]
        k = qkv[:, width + h * head : width + (h + 1) * head]
        v = qkv[:, 2 * width + h * head : 2 * width + (h + 1) * head]
        ga = grad_attended[:, h * head : (h + 1) * head]
        scores = jnp.where(keep, dot(q, k, NT) * scale, NEGATIVE)
        weights = jnp.exp(scores - lse[:, h : h + 1])
        grad_v.append(dot(weights.astype(bf16), ga, TN).astype(bf16))
        grad_weights = dot(ga, v, NT)
        row = jnp.sum(weights * grad_weights, axis=1, keepdims=True)
        grad_scores = (weights * (grad_weights - row)).astype(bf16)
        grad_q.append((dot(grad_scores, k) * scale).astype(bf16))
        grad_k.append((dot(grad_scores, q, TN) * scale).astype(bf16))
    grad_qkv = jnp.concatenate(grad_q + grad_k + grad_v, axis=1)
    hat_one, inverse_one = norm_rows(pad_rows(tok_ref[0].astype(f32), rows))
    normed = (hat_one * gains_ref[0:1, :]).astype(bf16)
    gqkv_ref[...] += dot(normed, grad_qkv, TN)
    grad_normed = dot(grad_qkv, pack_ref[:, 0 : 3 * width], NT)
    ggain[0:1, :] += jnp.sum(grad_normed * hat_one, axis=0, keepdims=True)
    grad_inputs = grad_residual + norm_back(grad_normed * gains_ref[0:1, :], hat_one, inverse_one)
    gtok_ref[0] = grad_inputs[: gtok_ref.shape[1]]

    @pl.when(step == images - 1)
    def _():
        zeros = jnp.zeros((GAIN_LANE, width), f32)
        tail = jnp.concatenate([zeros, ggain[...], zeros[: GAIN_LANE - 8]], axis=0)
        grest_ref[...] += tail.T


def backward(lay, tokens, mask, cotangent, code, qkv, att, res, lse, routed, probs, pack, gains, gx, gate):
    images, positions, width = tokens.shape
    rows = att.shape[1]
    slots = gate.shape[0] * gate.shape[2]
    return pl.pallas_call(
        functools.partial(backward_kernel, lay),
        grid=(images,),
        out_shape=(
            Shape((images, positions, width), f32),
            Shape((width, 3 * width), f32),
            Shape((width, width), f32),
            Shape((width, LANES), f32),
        ),
        in_specs=[
            per_image(positions, width),
            per_image(1, rows),
            per_image(positions, width),
            per_image(rows, 2),
            per_image(rows, 3 * width),
            per_image(rows, width),
            per_image(rows, width),
            per_image(rows, HEADS),
            per_image(rows, width),
            per_image(rows, LANES),
        ]
        + [vmem()] * 4,
        out_specs=(
            per_image(positions, width),
            fixed(width, 3 * width),
            fixed(width, width),
            fixed(width, LANES),
        ),
        scratch_shapes=[pltpu.VMEM((2 * LANES, slots), bf16), pltpu.VMEM((8, width), f32)],
        compiler_params=pltpu.CompilerParams(vmem_limit_bytes=VMEM_LIMIT),
        cost_estimate=pl.CostEstimate(flops=4 * 10**10, bytes_accessed=30 * 10**6, transcendentals=3 * 10**6),
    )(tokens, mask, cotangent, code, qkv, att, res, lse, routed, probs, pack, gains, gx, gate)


def mix_kernel(code_ref, res_ref, zy_ref, out_ref):
    members, cap, width = zy_ref.shape
    rows = res_ref.shape[1]
    code = code_ref[0]
    slot = lax.broadcasted_iota(jnp.int32, (rows, members * cap), 1)
    pick = jnp.where((code[:, 0:1] == slot) | (code[:, 1:2] == slot), 1.0, 0.0).astype(bf16)
    mixed = res_ref[0] + dot(pick, zy_ref[...].reshape(members * cap, width))
    out_ref[0] = mixed[: out_ref.shape[1]].astype(bf16)


def mix(positions, code, res, zy):
    images, rows, width = res.shape
    return pl.pallas_call(
        mix_kernel,
        grid=(images,),
        out_shape=Shape((images, positions, width), bf16),
        in_specs=[per_image(rows, 2), per_image(rows, width), vmem()],
        out_specs=per_image(positions, width),
        compiler_params=pltpu.CompilerParams(vmem_limit_bytes=VMEM_LIMIT),
        cost_estimate=pl.CostEstimate(flops=7 * 10**9, bytes_accessed=12 * 10**6, transcendentals=0),
    )(code, res, zy)


def body(
    lay, tokens, w_qkv, w_attn_out, w_router, gain_attn, gain_moe, w_expert_in, w_expert_down, key_mask,
    expert_choice, slot_index, cotangent,
):
    images, positions, width = tokens.shape
    N, S, L = lay.N, lay.S, lay.L
    experts = w_router.shape[1]
    rows = -(-positions // 16) * 16
    token_rows = images * positions
    capacity = ((token_rows * 10 + 4 * experts - 1) // (4 * experts) + 7) // 8 * 8
    dp, s, g, l = lay.here()

    def place(g, l, s):
        return (g * L + l) * S + s

    def route(j):
        pairs = []
        for gg in range(S):
            for ll in range(L):
                for ss in range(S):
                    d = (ss + j) % S
                    pairs.append((place(gg, ll, ss), place((gg - d) % S, ll, (d - ll) % S)))
        return pairs

    weights = []
    for j in range(S):
        weights.append(lax.ppermute(w_expert_in, ("dp", "seq"), route(j)))
        weights.append(lax.ppermute(w_expert_down, ("dp", "seq"), route(j)))

    height = w_qkv.shape[0]
    lane = jnp.arange(LANES, dtype=jnp.int32)[None, :]
    rest = jnp.pad(w_router, ((0, 0), (0, LANES - experts)))
    rest = jnp.where(lane == GAIN_LANE, gain_attn[:, None], jnp.where(lane == GAIN_LANE + 1, gain_moe[:, None], rest))
    own = jnp.concatenate([w_qkv, w_attn_out, rest], axis=1)
    if height % 16:
        own = lax.all_gather(own, "seq", axis=0, tiled=True)
        carrier = Rows(N, 1)
    else:
        carrier = Rows(N, S)
    pack = gather_rows(carrier, own)
    gains = pack[:, 4 * width + GAIN_LANE : 4 * width + GAIN_LANE + 8].T.astype(f32)

    mask = lax.dynamic_slice_in_dim(key_mask, s * images, images, axis=0)
    mask = jnp.pad(mask, ((0, 0), (0, rows - positions)))[:, None, :]
    group, local = expert_choice // L, lax.rem(expert_choice, L)
    member = local * S + lax.rem(group - g - local + (L + 1) * S, S)
    code = jnp.where(slot_index >= 0, member * capacity + slot_index, -1)
    code = jnp.pad(code, ((0, 0), (0, rows - positions), (0, 0)), constant_values=-1)
    code_rows = code.reshape(images * rows, 2).T

    qkv, att, res, lse, routed, probs = forward(experts, rows, tokens, mask, pack, gains)
    router = pack[:, 4 * width :]
    gx, zy, gate, gwi, gwd = run_experts(lay, experts, capacity, routed, cotangent, code_rows, router, weights)

    sums = []
    for partial in (gwi, gwd):
        total = None
        for j in range(S):
            back = [(b, a) for a, b in route(j)]
            part = lax.ppermute(partial[j : j + 1], ("dp", "seq"), back).astype(f32)
            total = part if total is None else total + part
        sums.append(total)

    gtok, gqkv, gout, grest = backward(
        lay, tokens, mask, cotangent, code, qkv, att, res, lse, routed, probs, pack, gains, gx, gate
    )
    mixed = mix(positions, code, res, zy)
    own = scatter_rows(carrier, gqkv, gout, grest)
    if height % 16:
        own = lax.psum_scatter(own, "seq", scatter_dimension=0, tiled=True)
    rest = own[:, 4 * width :]
    return (
        mixed,
        gtok,
        own[:, : 3 * width],
        own[:, 3 * width : 4 * width],
        rest[:, :experts],
        rest[:, GAIN_LANE],
        rest[:, GAIN_LANE + 1],
        sums[0],
        sums[1],
    )


def solution(mesh):
    lay = Layout(mesh.shape["dp"], mesh.shape["seq"])
    return jax.shard_map(
        functools.partial(body, lay),
        mesh=mesh,
        in_specs=(
            P(("dp", "seq"), None, None),
            P(("dp", "seq"), None),
            P(("dp", "seq"), None),
            P(("dp", "seq"), None),
            P(("dp", "seq")),
            P(("dp", "seq")),
            P("dp", "seq", None),
            P("dp", "seq", None),
            P("dp", None),
            P(("dp", "seq"), None, None),
            P(("dp", "seq"), None, None),
            P(("dp", "seq"), None, None),
        ),
        out_specs=(
            P(("dp", "seq"), None, None),
            P(("dp", "seq"), None, None),
            P(("dp", "seq"), None),
            P(("dp", "seq"), None),
            P(("dp", "seq"), None),
            P(("dp", "seq")),
            P(("dp", "seq")),
            P("dp", "seq", None),
            P("dp", "seq", None),
        ),
        check_vma=False,
    )
```

```python
import functools

import jax
import jax.numpy as jnp
from jax import lax
from jax.experimental import pallas as pl
from jax.experimental.pallas import tpu as pltpu
from jax.sharding import PartitionSpec as P

HEADS = 8
EPSILON = 1e-06
NEGATIVE = -1e30
MESH = pl.DeviceIdType.MESH
bf16, f32 = jnp.bfloat16, jnp.float32
NN = (((1,), (0,)), ((), ()))
NT = (((1,), (1,)), ((), ()))
TN = (((0,), (0,)), ((), ()))
LANES = 128
GAIN_LANE = 64
VMEM_LIMIT = 60 << 20
Shape = jax.ShapeDtypeStruct


def dot(a, b, dims=NN):
    return lax.dot_general(a, b, dims, preferred_element_type=f32)


def pad_rows(values, rows):
    extra = rows - values.shape[0]
    if extra == 0:
        return values
    return jnp.concatenate([values, jnp.zeros((extra, values.shape[1]), values.dtype)], axis=0)


def norm_rows(values):
    centred = values - jnp.mean(values, axis=-1, keepdims=True)
    inverse = lax.rsqrt(jnp.mean(centred * centred, axis=-1, keepdims=True) + EPSILON)
    return centred * inverse, inverse


def norm_back(grad_hat, normed, inverse):
    return inverse * (
        grad_hat
        - jnp.mean(grad_hat, axis=-1, keepdims=True)
        - normed * jnp.mean(grad_hat * normed, axis=-1, keepdims=True)
    )


def router_softmax(logits, experts):
    lane = lax.broadcasted_iota(jnp.int32, logits.shape, 1)
    logits = jnp.where(lane < experts, logits, NEGATIVE)
    exps = jnp.exp(logits - jnp.max(logits, axis=1, keepdims=True))
    return exps / jnp.sum(exps, axis=1, keepdims=True)


def gelu_parts(inner):
    k, c = 0.7978845608028654, 0.044715
    square = inner * inner
    t = jnp.tanh(inner * (k + (k * c) * square))
    half = 0.5 + 0.5 * t
    value = inner * half
    slope = half + value * (1.0 - half) * (2 * k + (6 * k * c) * square)
    return value, slope


def anywhere():
    return pl.BlockSpec(memory_space=pl.ANY)


def per_image(*dims):
    return pl.BlockSpec((1,) + dims, lambda i: (i,) + (0,) * len(dims))


def fixed(*dims):
    return pl.BlockSpec(dims, lambda i: (0,) * len(dims), pipeline_mode=pl.Buffered(1))


class Layout:
    def __init__(self, dp, seq):
        self.N, self.S = dp, seq
        self.L = dp // seq

    def here(self):
        dp, s = lax.axis_index("dp"), lax.axis_index("seq")
        return dp, s, dp // self.L, lax.rem(dp, self.L)

    def member_device(self, g, m):
        return (g * self.L + m // self.S, lax.rem(m, self.S))

    def group_peers(self):
        _, s, g, l = self.here()
        return [self.member_device(g, jnp.bitwise_xor(l * self.S + s, k)) for k in range(1, self.N)]

    def weight_peers(self):
        _, s, g, l = self.here()
        count = self.S * self.S
        places = [lax.rem(g * self.S + s + i, count) for i in range(1, count)]
        return [(q // self.S * self.L + l, lax.rem(q, self.S)) for q in places]

    def expert_of(self, g, m):
        l, s = m // self.S, lax.rem(m, self.S)
        return lax.rem(g + s + l, self.S) * self.L + l


def greet(peers):
    barrier = pltpu.get_barrier_semaphore()
    for peer in peers:
        pl.semaphore_signal(barrier, inc=1, device_id=peer, device_id_type=MESH)
    pl.semaphore_wait(barrier, len(peers))


class Rows:
    def __init__(self, dp, seq):
        self.A, self.S = dp // 4, seq

    def here(self):
        dp, s = lax.axis_index("dp"), lax.axis_index("seq")
        return dp // 4, lax.rem(dp // 2, 2), lax.rem(dp, 2), s

    def device(self, a, b, c, s):
        return ((a * 2 + b) * 2 + c, s)

    def along_a(self):
        a, b, c, s = self.here()
        return [(i, lax.rem(a + i, self.A)) for i in range(1, self.A)]

    def plane(self):
        a, b, c, s = self.here()
        for i in range(1, 2 * self.S):
            if self.S == 1:
                yield i, 1 - b, s, 0
            else:
                q = lax.rem(b * self.S + s + i, 2 * self.S)
                yield i, q // self.S, lax.rem(q, self.S), lax.rem(q, self.S)


def attend(heads, qkv, keep, width):
    head = width // heads
    outs, lses = [], []
    for h in range(heads):
        q = qkv[:, h * head : (h + 1) * head]
        k = qkv[:, width + h * head : width + (h + 1) * head]
        v = qkv[:, 2 * width + h * head : 2 * width + (h + 1) * head]
        scores = jnp.where(keep, dot(q, k, NT) * (head**-0.5), NEGATIVE)
        row_max = jnp.max(scores, axis=1, keepdims=True)
        exps = jnp.exp(scores - row_max)
        totals = jnp.sum(exps, axis=1, keepdims=True)
        lses.append(row_max + jnp.log(totals))
        outs.append(dot((exps / totals).astype(bf16), v).astype(bf16))
    return jnp.concatenate(outs, axis=1), jnp.concatenate(lses, axis=1)


def front_kernel(
    lay, rows, experts,
    own_ref, tok_ref, mask_ref, cot_ref, code_ref, w_in_ref, w_down_ref,
    pack_ref, gains_ref, qkv_ref, att_ref, res_ref, lse_ref, routed_ref, probs_ref,
    gx_ref, zy_ref, gate_ref, gwi_ref, gwd_ref,
    full, routed, cot, w_in, w_down, x_send, c_send, x_recv, c_recv, gate_send, gwi, gwd,
    ps, pr, ws, wr, xs, xr, cs, cr, gs, gr, ts, tr, zs, ls,
):
    step = pl.program_id(0)
    steps = pl.num_programs(0)
    a, b, c, s = rows.here()
    _, _, g, l = lay.here()
    S, L = lay.S, lay.L
    members, cap, width = x_send.shape
    images, height = routed.shape[0], routed.shape[1]
    me = l * S + s
    delta = lax.rem(s + l, S)
    part_rows = w_in.shape[0] // S

    def remote(src, dst, send, recv, device):
        return pltpu.make_async_remote_copy(src, dst, send, recv, device_id=device, device_id_type=MESH)

    def to_member(src, dst, send, recv, k):
        return remote(src, dst, send.at[k], recv.at[k], lay.member_device(g, jnp.bitwise_xor(me, k)))

    def x_copy(k):
        return to_member(x_send.at[jnp.bitwise_xor(me, k)], x_recv.at[me], xs, xr, k)

    def c_copy(k):
        return to_member(c_send.at[jnp.bitwise_xor(me, k)], c_recv.at[me], cs, cr, k)

    def gx_copy(k):
        return to_member(c_send.at[jnp.bitwise_xor(me, k)], gx_ref.at[me], gs, gr, k)

    def gate_copy(k):
        return to_member(gate_send.at[jnp.bitwise_xor(me, k)], gate_ref.at[me], ts, tr, k)

    def zy_copy(k):
        m = jnp.bitwise_xor(me, k)
        return pltpu.make_async_copy(x_send.at[m], zy_ref.at[m], zs.at[k])

    def pick_rows(m, values, target):
        slot = lax.broadcasted_iota(jnp.int32, (cap, images * height), 0) + m * cap
        hit = (code_ref[0:1, :] == slot) | (code_ref[1:2, :] == slot)
        pick = jnp.where(hit, 1.0, 0.0).astype(bf16)
        target[m] = dot(pick, values[...].reshape(images * height, width)).astype(bf16)

    def build_c(first, last):
        def build(k, carry):
            pick_rows(jnp.bitwise_xor(me, k), cot, c_send)
            return carry

        lax.fori_loop(first, last, build, 0)

    def weight_copies(d):
        device = (lax.rem(g - d + S, S) * L + l, lax.rem(d - l + L * S, S))
        mine = pl.ds(pl.multiple_of(s * part_rows, part_rows), part_rows)
        return [
            remote(src.at[0], dst.at[mine], ws.at[2 * d + i], wr.at[2 * s + i], device)
            for i, (src, dst) in enumerate(((w_in_ref, w_in), (w_down_ref, w_down)))
        ]

    def weight_local():
        mine = pl.ds(pl.multiple_of(s * part_rows, part_rows), part_rows)
        return [
            pltpu.make_async_copy(src.at[0], dst.at[mine], wr.at[2 * s + i])
            for i, (src, dst) in enumerate(((w_in_ref, w_in), (w_down_ref, w_down)))
        ]

    @pl.when(step == 0)
    def _():
        greet(
            [rows.device(i, b, c, s) for _, i in rows.along_a()]
            + [rows.device(a, b2, c, s2) for _, b2, s2, _ in rows.plane()]
            + [rows.device(a, b, 1 - c, s)]
            + lay.group_peers()
            + lay.weight_peers()
        )
        A, Q = rows.A, 2 * rows.S
        sl = s if rows.S > 1 else 0
        third = members // 3
        local = pltpu.make_async_copy(own_ref, full.at[a, b, c, sl], ls.at[0])
        local.start()
        copies = [
            remote(own_ref, full.at[a, b, c, sl], ps.at[i], pr.at[i], rows.device(a2, b, c, s))
            for i, a2 in rows.along_a()
        ]
        for copy in copies:
            copy.start()
        for i in range(images):
            cot[i] = pad_rows(cot_ref[i].astype(f32), height).astype(bf16)
        build_c(0, third)
        local.wait()
        for copy in copies:
            copy.wait()
        copies = [
            remote(
                full.at[:, b, c, sl], full.at[:, b, c, sl], ps.at[A + i], pr.at[A + i], rows.device(a, b2, c, s2)
            )
            for i, b2, s2, _ in rows.plane()
        ]
        for copy in copies:
            copy.start()
        build_c(third, members)
        for copy in copies:
            copy.wait()
        last = remote(
            full.at[:, :, c], full.at[:, :, c], ps.at[A + Q], pr.at[A + Q], rows.device(a, b, 1 - c, s)
        )
        last.start()
        for d in range(1, S):
            for copy in weight_copies(d):
                copy.start()

        @pl.when(delta == 0)
        def _():
            for copy in weight_local():
                copy.start()

        @pl.when(delta != 0)
        def _():
            for copy in weight_copies(0):
                copy.start()

        def send(k, carry):
            c_copy(k).start()
            return carry

        lax.fori_loop(1, members, send, 0)
        c_recv[me] = c_send[me]
        last.wait()
        pack_ref[...] = full[...].reshape(pack_ref.shape)
        tail = pack_ref[:, 4 * width :].astype(f32).T
        gains_ref[...] = tail[GAIN_LANE : GAIN_LANE + 8, :]

    inputs = pad_rows(tok_ref[0].astype(f32), height)
    hat, _ = norm_rows(inputs)
    normed = (hat * gains_ref[0:1, :]).astype(bf16)
    qkv = dot(normed, pack_ref[:, 0 : 3 * width]).astype(bf16)
    qkv_ref[0] = qkv
    att, lse = attend(HEADS, qkv, mask_ref[0] > 0, width)
    att_ref[0] = att
    lse_ref[0] = lse
    residual = inputs + dot(att, pack_ref[:, 3 * width : 4 * width])
    res_ref[0] = residual
    hat, _ = norm_rows(residual)
    routed_now = (hat * gains_ref[1:2, :]).astype(bf16)
    routed_ref[0] = routed_now
    routed[step] = routed_now
    probs_ref[0] = router_softmax(dot(routed_now, pack_ref[:, 4 * width :]), experts)

    @pl.when(step == steps - 1)
    def _():
        def dispatch(k, carry):
            pick_rows(jnp.bitwise_xor(me, k), routed, x_send)

            @pl.when(k > 0)
            def _():
                x_copy(k).start()

            return carry

        lax.fori_loop(0, members, dispatch, 0)
        x_recv[me] = x_send[me]
        gwi[...] = jnp.zeros_like(gwi)
        gwd[...] = jnp.zeros_like(gwd)

        for p in range(S):
            for copy_in in range(2):
                span = pl.ds(p * part_rows, part_rows)
                dst = (w_in, w_down)[copy_in].at[span]
                src = (w_in_ref, w_down_ref)[copy_in].at[0]

                @pl.when((delta == 0) & (s == p))
                def _():
                    pltpu.make_async_copy(src, dst, wr.at[2 * p + copy_in]).wait()

                @pl.when((delta != 0) | (s != p))
                def _():
                    remote(src, dst, ws.at[0], wr.at[2 * p + copy_in], (0, 0)).wait_recv()

        mine = lay.expert_of(g, me)
        hidden = w_in.shape[1]
        chunk = min(512, hidden)

        def work(j, carry):
            ks = (2 * j, 2 * j + 1)
            ms = [jnp.bitwise_xor(me, k) for k in ks]

            @pl.when(j > 0)
            def _():
                x_copy(ks[0]).wait()
                c_copy(ks[0]).wait()

            x_copy(ks[1]).wait()
            c_copy(ks[1]).wait()
            x = jnp.concatenate([x_recv[m] for m in ms], axis=0)
            cf = jnp.concatenate([c_recv[m] for m in ms], axis=0).astype(f32)
            probs = router_softmax(dot(x, pack_ref[:, 4 * width :]), experts)
            lane = lax.broadcasted_iota(jnp.int32, probs.shape, 1)
            gate = jnp.sum(jnp.where(lane == mine, probs, 0.0), axis=1, keepdims=True)
            dy = (gate * cf).astype(bf16)
            y, gx = None, None
            for f in range(0, hidden, chunk):
                span = slice(f, f + chunk)
                value, slope = gelu_parts(dot(x, w_in[:, span]))
                act = value.astype(bf16)
                inner_grad = (dot(dy, w_down[:, span]) * slope).astype(bf16)
                y_part, gx_part = dot(act, w_down[:, span], NT), dot(inner_grad, w_in[:, span], NT)
                y = y_part if y is None else y + y_part
                gx = gx_part if gx is None else gx + gx_part
                gwd[:, span] += dot(dy, act, TN)
                gwi[:, span] += dot(x, inner_grad, TN)
            zy = (gate * y).astype(bf16)
            gxb = gx.astype(bf16)
            gate_grad = jnp.broadcast_to(jnp.sum(y * cf, axis=1, keepdims=True), (2 * cap, LANES)).T
            for q in range(2):
                c_send[ms[q]] = gxb[q * cap : (q + 1) * cap]
                x_send[ms[q]] = zy[q * cap : (q + 1) * cap]
                gate_send[ms[q]] = gate_grad[0:8, q * cap : (q + 1) * cap]

            @pl.when(j > 0)
            def _():
                gx_copy(ks[0]).start()
                gate_copy(ks[0]).start()

            gx_copy(ks[1]).start()
            gate_copy(ks[1]).start()
            zy_copy(ks[0]).start()
            zy_copy(ks[1]).start()
            return carry

        lax.fori_loop(0, members // 2, work, 0)
        keeps = [
            pltpu.make_async_copy(c_send.at[me], gx_ref.at[me], ls.at[0]),
            pltpu.make_async_copy(gate_send.at[me], gate_ref.at[me], ls.at[1]),
        ]
        for keep in keeps:
            keep.start()
        gwi_ref[...] = gwi[...].astype(bf16)
        gwd_ref[...] = gwd[...].astype(bf16)
        for keep in keeps:
            keep.wait()
        zy_copy(0).wait()
        for d in range(1, S):
            for copy in weight_copies(d):
                copy.wait_send()

        @pl.when(delta != 0)
        def _():
            for copy in weight_copies(0):
                copy.wait_send()

        def finish(k, carry):
            gx_copy(k).wait()
            gate_copy(k).wait()
            zy_copy(k).wait()
            return carry

        lax.fori_loop(1, members, finish, 0)


def front(lay, rows, experts, cap, own, tokens, mask, cotangent, codes, w_in, w_down):
    S, M = lay.S, lay.N
    images, positions, width = tokens.shape
    height = mask.shape[2]
    hidden = w_in.shape[-1]
    blocks = (M, cap, width)
    full = (rows.A, 2, 2, rows.S) + own.shape
    total = rows.A * 4 * rows.S * own.shape[0]
    dma = lambda n: pltpu.SemaphoreType.DMA((n,))
    count = rows.A + 2 * rows.S + 1
    return pl.pallas_call(
        functools.partial(front_kernel, lay, rows, experts),
        grid=(images,),
        out_shape=(
            Shape((total, own.shape[1]), bf16),
            Shape((8, width), f32),
            Shape((images, height, 3 * width), bf16),
            Shape((images, height, width), bf16),
            Shape((images, height, width), f32),
            Shape((images, height, HEADS), f32),
            Shape((images, height, width), bf16),
            Shape((images, height, LANES), f32),
            Shape(blocks, bf16),
            Shape(blocks, bf16),
            Shape((M, 8, cap), f32),
            Shape((width, hidden), bf16),
            Shape((width, hidden), bf16),
        ),
        in_specs=[
            fixed(*own.shape),
            per_image(positions, width),
            per_image(1, height),
            fixed(*cotangent.shape),
            fixed(*codes.shape),
            anywhere(),
            anywhere(),
        ],
        out_specs=(
            fixed(total, own.shape[1]),
            fixed(8, width),
            per_image(height, 3 * width),
            per_image(height, width),
            per_image(height, width),
            per_image(height, HEADS),
            per_image(height, width),
            per_image(height, LANES),
            anywhere(),
            anywhere(),
            anywhere(),
            fixed(width, hidden),
            fixed(width, hidden),
        ),
        scratch_shapes=[
            pltpu.VMEM(full, bf16),
            pltpu.VMEM((images, height, width), bf16),
            pltpu.VMEM((images, height, width), bf16),
            pltpu.VMEM((width, hidden), bf16),
            pltpu.VMEM((width, hidden), bf16),
            *[pltpu.VMEM(blocks, bf16)] * 4,
            pltpu.VMEM((M, 8, cap), f32),
            pltpu.VMEM((width, hidden), f32),
            pltpu.VMEM((width, hidden), f32),
            dma(count), dma(count), dma(2 * S), dma(2 * S),
            *[dma(M)] * 9,
            dma(2),
        ],
        compiler_params=pltpu.CompilerParams(
            collective_id=0, has_side_effects=True, vmem_limit_bytes=VMEM_LIMIT, dimension_semantics=("arbitrary",)
        ),
    )(own, tokens, mask, cotangent, codes, w_in, w_down)


def back_kernel(
    lay, rows,
    tok_ref, mask_ref, cot_ref, code_ref, qkv_ref, att_ref, res_ref, lse_ref, routed_ref, probs_ref,
    pack_ref, gains_ref, gx_ref, gate_ref, zy_ref, gwi_ref, gwd_ref,
    gtok_ref, mixed_ref, own_ref, gwi_parts, gwd_parts,
    gqkv, gout, grest, table, ggain, residuals, codes, zy, part, recv1, sum1, recv2, sum2, recv3,
    ps, pr, zs, zr, ws, wr, ls,
):
    step = pl.program_id(0)
    images = pl.num_programs(0)
    a, b, c, s = rows.here()
    _, _, g, l = lay.here()
    S, L = lay.S, lay.L
    me = l * S + s
    delta = lax.rem(s + l, S)
    members, _, cap = gate_ref.shape
    slots = members * cap
    height, width = att_ref.shape[1], att_ref.shape[2]
    positions = gtok_ref.shape[1]
    head = width // HEADS
    part_rows = gwi_ref.shape[0] // S

    def remote(src, dst, send, recv, device):
        return pltpu.make_async_remote_copy(src, dst, send, recv, device_id=device, device_id_type=MESH)

    def zy_copy(k):
        m = jnp.bitwise_xor(me, k)
        return remote(zy_ref.at[m], zy.at[me], zs.at[k], zr.at[k], lay.member_device(g, m))

    owner = lax.rem(g + delta, S)

    def weight_pairs(p):
        span = pl.ds(p * part_rows, part_rows)
        return ((gwi_ref.at[span], gwi_parts.at[g]), (gwd_ref.at[span], gwd_parts.at[g]))

    def weight_copies(p):
        return [
            remote(src, dst, ws.at[2 * p + i], wr.at[2 * g + i], (owner * L + l, p))
            for i, (src, dst) in enumerate(weight_pairs(p))
        ]

    def weight_local(p):
        return [
            pltpu.make_async_copy(src, dst, ws.at[2 * p + i]) for i, (src, dst) in enumerate(weight_pairs(p))
        ]

    def for_parts(remote_do, local_do):
        for p in range(S):
            @pl.when((delta == 0) & (s == p))
            def _():
                for copy in weight_local(p):
                    local_do(copy)

            @pl.when((delta != 0) | (s != p))
            def _():
                for copy in weight_copies(p):
                    remote_do(copy)

    zy_keep = pltpu.make_async_copy(zy_ref.at[me], zy.at[me], ls.at[0])

    @pl.when(step == 0)
    def _():
        greet(
            [rows.device(i, b, c, s) for _, i in rows.along_a()]
            + [rows.device(a, b2, c, s2) for _, b2, s2, _ in rows.plane()]
            + [rows.device(a, b, 1 - c, s)]
            + lay.group_peers()
            + lay.weight_peers()
        )
        for_parts(lambda copy: copy.start(), lambda copy: copy.start())

        def send(k, carry):
            zy_copy(k).start()
            return carry

        lax.fori_loop(1, members, send, 0)
        zy_keep.start()
        for ref in (gqkv, gout, grest, ggain):
            ref[...] = jnp.zeros_like(ref)
        for m in range(members):
            values = gate_ref[m][0:1, :]
            high = values.astype(bf16).astype(f32)
            sub = lax.broadcasted_iota(jnp.int32, (LANES, cap), 0)
            here = sub == lay.expert_of(g, jnp.int32(m))
            span = slice(m * cap, (m + 1) * cap)
            table[0:LANES, span] = jnp.where(here, high, 0.0).astype(bf16)
            table[LANES : 2 * LANES, span] = jnp.where(here, values - high, 0.0).astype(bf16)

    def pick_slots(code):
        slot = lax.broadcasted_iota(jnp.int32, (height, slots), 1)
        return jnp.where((code[:, 0:1] == slot) | (code[:, 1:2] == slot), 1.0, 0.0).astype(bf16)

    code = code_ref[0]
    codes[step] = code
    residuals[step] = res_ref[0]
    pick = pick_slots(code)
    grad_routed = dot(pick, gx_ref[...].reshape(slots, width))
    both = dot(pick, table[...], NT)
    grad_probs = both[:, :LANES] + both[:, LANES:]
    probs = probs_ref[0]
    grad_logits = probs * (grad_probs - jnp.sum(grad_probs * probs, axis=1, keepdims=True))
    logit_high = grad_logits.astype(bf16)
    logit_low = (grad_logits - logit_high.astype(f32)).astype(bf16)
    router = pack_ref[:, 4 * width :]
    grad_router = dot(routed_ref[0], jnp.concatenate([logit_high, logit_low], axis=1), TN)
    grest[...] += grad_router[:, :LANES] + grad_router[:, LANES:]
    grad_routed += dot(logit_high, router, NT) + dot(logit_low, router, NT)
    hat_two, inverse_two = norm_rows(res_ref[0])
    ggain[1:2, :] += jnp.sum(grad_routed * hat_two, axis=0, keepdims=True)
    grad_residual = pad_rows(cot_ref[0].astype(f32), height) + norm_back(
        grad_routed * gains_ref[1:2, :], hat_two, inverse_two
    )
    grad_att = grad_residual.astype(bf16)
    gout[...] += dot(att_ref[0], grad_att, TN)
    grad_attended = dot(grad_att, pack_ref[:, 3 * width : 4 * width], NT).astype(bf16)
    keep = mask_ref[0] > 0
    qkv, lse = qkv_ref[0], lse_ref[0]
    scale = head**-0.5
    grad_q, grad_k, grad_v = [], [], []
    for h in range(HEADS):
        q = qkv[:, h * head : (h + 1) * head]
        k = qkv[:, width + h * head : width + (h + 1) * head]
        v = qkv[:, 2 * width + h * head : 2 * width + (h + 1) * head]
        ga = grad_attended[:, h * head : (h + 1) * head]
        scores = jnp.where(keep, dot(q, k, NT) * scale, NEGATIVE)
        weights = jnp.exp(scores - lse[:, h : h + 1])
        grad_v.append(dot(weights.astype(bf16), ga, TN).astype(bf16))
        grad_weights = dot(ga, v, NT)
        row = jnp.sum(weights * grad_weights, axis=1, keepdims=True)
        grad_scores = (weights * (grad_weights - row)).astype(bf16)
        grad_q.append((dot(grad_scores, k) * scale).astype(bf16))
        grad_k.append((dot(grad_scores, q, TN) * scale).astype(bf16))
    grad_qkv = jnp.concatenate(grad_q + grad_k + grad_v, axis=1)
    hat_one, inverse_one = norm_rows(pad_rows(tok_ref[0].astype(f32), height))
    normed = (hat_one * gains_ref[0:1, :]).astype(bf16)
    gqkv[...] += dot(normed, grad_qkv, TN)
    grad_normed = dot(grad_qkv, pack_ref[:, 0 : 3 * width], NT)
    ggain[0:1, :] += jnp.sum(grad_normed * hat_one, axis=0, keepdims=True)
    grad_inputs = grad_residual + norm_back(grad_normed * gains_ref[0:1, :], hat_one, inverse_one)
    gtok_ref[0] = grad_inputs[:positions]

    @pl.when(step == images - 1)
    def _():
        A, Q = rows.A, 2 * rows.S
        zeros = jnp.zeros((GAIN_LANE, width), f32)
        tail = jnp.concatenate([zeros, ggain[...], zeros[: GAIN_LANE - 8]], axis=0)
        grest[...] += tail.T
        shape = part.shape[:5]
        part[..., 0 : 3 * width] = gqkv[...].astype(bf16).reshape(shape + (3 * width,))
        part[..., 3 * width : 4 * width] = gout[...].astype(bf16).reshape(shape + (width,))
        part[..., 4 * width :] = grest[...].astype(bf16).reshape(shape + (LANES,))
        first = remote(part.at[:, :, 1 - c], recv1, ps.at[0], pr.at[0], rows.device(a, b, 1 - c, s))
        first.start()

        def wait_zy(k, carry):
            zy_copy(k).wait()
            return carry

        lax.fori_loop(1, members, wait_zy, 0)
        zy_keep.wait()

        def mix(first_image, last_image):
            def one(i, carry):
                mixed = residuals[i] + dot(pick_slots(codes[i]), zy[...].reshape(slots, width))
                mixed_ref[i] = mixed[:positions].astype(bf16)
                return carry

            lax.fori_loop(first_image, last_image, one, 0)

        count = residuals.shape[0]
        mix(0, count // 4)
        first.wait()
        sum1[...] = (part[:, :, c].astype(f32) + recv1[...].astype(f32)).astype(bf16)
        copies = [
            remote(sum1.at[:, b2, sl2], recv2.at[i - 1], ps.at[i], pr.at[i], rows.device(a, b2, c, s2))
            for i, b2, s2, sl2 in rows.plane()
        ]
        for copy in copies:
            copy.start()
        mix(count // 4, count * 3 // 4)
        for copy in copies:
            copy.wait()
        sl = s if rows.S > 1 else 0
        total = sum1[:, b, sl].astype(f32)
        for i in range(Q - 1):
            total += recv2[i].astype(f32)
        sum2[...] = total.astype(bf16)
        copies = [
            remote(sum2.at[a2], recv3.at[i - 1], ps.at[Q + i], pr.at[Q + i], rows.device(a2, b, c, s))
            for i, a2 in rows.along_a()
        ]
        for copy in copies:
            copy.start()
        mix(count * 3 // 4, count)
        for copy in copies:
            copy.wait()
        final = sum2[a].astype(f32)
        for i in range(A - 1):
            final += recv3[i].astype(f32)
        own_ref[...] = final

        for_parts(lambda copy: copy.wait_send(), lambda copy: copy.wait())
        for q in range(S):
            @pl.when((delta != 0) | (g != q))
            def _():
                for i, (src, dst) in enumerate(((gwi_ref, gwi_parts), (gwd_ref, gwd_parts))):
                    span = pl.ds(0, part_rows)
                    remote(src.at[span], dst.at[q], ws.at[i], wr.at[2 * q + i], (0, 0)).wait_recv()


def back(
    lay, rows, own_height, tokens, mask, cotangent, code, qkv, att, res, lse, routed, probs, pack, gains, gx, gate,
    zy, gwi, gwd,
):
    images, positions, width = tokens.shape
    height = att.shape[1]
    M, _, cap = gate.shape
    slots = M * cap
    A, S = rows.A, rows.S
    G = lay.S
    hidden = gwi.shape[1]
    part_rows = gwi.shape[0] // G
    columns = pack.shape[1]
    dma = lambda n: pltpu.SemaphoreType.DMA((n,))
    count = A + 2 * S + 1
    return pl.pallas_call(
        functools.partial(back_kernel, lay, rows),
        grid=(images,),
        out_shape=(
            Shape((images, positions, width), f32),
            Shape((images, positions, width), bf16),
            Shape((own_height, columns), f32),
            Shape((G, part_rows, hidden), bf16),
            Shape((G, part_rows, hidden), bf16),
        ),
        in_specs=[
            per_image(positions, width),
            per_image(1, height),
            per_image(positions, width),
            per_image(height, 2),
            per_image(height, 3 * width),
            per_image(height, width),
            per_image(height, width),
            per_image(height, HEADS),
            per_image(height, width),
            per_image(height, LANES),
            fixed(*pack.shape),
            fixed(*gains.shape),
            fixed(*gx.shape),
            fixed(*gate.shape),
            anywhere(),
            anywhere(),
            anywhere(),
        ],
        out_specs=(
            per_image(positions, width),
            fixed(images, positions, width),
            fixed(own_height, columns),
            anywhere(),
            anywhere(),
        ),
        scratch_shapes=[
            pltpu.VMEM((width, 3 * width), f32),
            pltpu.VMEM((width, width), f32),
            pltpu.VMEM((width, LANES), f32),
            pltpu.VMEM((2 * LANES, slots), bf16),
            pltpu.VMEM((8, width), f32),
            pltpu.VMEM((images, height, width), f32),
            pltpu.VMEM((images, height, 2), jnp.int32),
            pltpu.VMEM((M, cap, width), bf16),
            pltpu.VMEM((A, 2, 2, S, own_height, columns), bf16),
            pltpu.VMEM((A, 2, S, own_height, columns), bf16),
            pltpu.VMEM((A, 2, S, own_height, columns), bf16),
            pltpu.VMEM((2 * S - 1, A, own_height, columns), bf16),
            pltpu.VMEM((A, own_height, columns), bf16),
            pltpu.VMEM((A - 1, own_height, columns), bf16),
            dma(count), dma(count), dma(M), dma(M), dma(2 * G), dma(2 * G), dma(1),
        ],
        compiler_params=pltpu.CompilerParams(
            collective_id=1, has_side_effects=True, vmem_limit_bytes=VMEM_LIMIT, dimension_semantics=("arbitrary",)
        ),
    )(tokens, mask, cotangent, code, qkv, att, res, lse, routed, probs, pack, gains, gx, gate, zy, gwi, gwd)


def body(
    lay, tokens, w_qkv, w_attn_out, w_router, gain_attn, gain_moe, w_expert_in, w_expert_down, key_mask,
    expert_choice, slot_index, cotangent,
):
    images, positions, width = tokens.shape
    N, S, L = lay.N, lay.S, lay.L
    experts = w_router.shape[1]
    height = -(-positions // 16) * 16
    token_rows = images * positions
    capacity = ((token_rows * 10 + 4 * experts - 1) // (4 * experts) + 7) // 8 * 8
    dp, s, g, l = lay.here()

    lane = jnp.arange(LANES, dtype=jnp.int32)[None, :]
    rest = jnp.pad(w_router, ((0, 0), (0, LANES - experts)))
    rest = jnp.where(lane == GAIN_LANE, gain_attn[:, None], jnp.where(lane == GAIN_LANE + 1, gain_moe[:, None], rest))
    own = jnp.concatenate([w_qkv, w_attn_out, rest], axis=1)
    few = w_qkv.shape[0] % 16 != 0
    if few:
        own = lax.all_gather(own, "seq", axis=0, tiled=True)
    rows = Rows(N, 1 if few else S)

    mask = lax.dynamic_slice_in_dim(key_mask, s * images, images, axis=0)
    mask = jnp.pad(mask, ((0, 0), (0, height - positions)))[:, None, :]
    group, local = expert_choice // L, lax.rem(expert_choice, L)
    member = local * S + lax.rem(group - g - local + (L + 1) * S, S)
    code = jnp.where(slot_index >= 0, member * capacity + slot_index, -1)
    code = jnp.pad(code, ((0, 0), (0, height - positions), (0, 0)), constant_values=-1)
    code_rows = code.reshape(images * height, 2).T

    pack, gains, qkv, att, res, lse, routed, probs, gx, zy, gate, gwi, gwd = front(
        lay, rows, experts, capacity, own, tokens, mask, cotangent, code_rows, w_expert_in, w_expert_down
    )
    gtok, mixed, sums, gwi, gwd = back(
        lay, rows, own.shape[0], tokens, mask, cotangent, code, qkv, att, res, lse, routed, probs, pack, gains, gx,
        gate, zy, gwi, gwd,
    )
    if few:
        sums = lax.psum_scatter(sums, "seq", scatter_dimension=0, tiled=True)
    rest = sums[:, 4 * width :]
    return (
        mixed,
        gtok,
        sums[:, : 3 * width],
        sums[:, 3 * width : 4 * width],
        rest[:, :experts],
        rest[:, GAIN_LANE],
        rest[:, GAIN_LANE + 1],
        jnp.sum(gwi.astype(f32), axis=0, keepdims=True),
        jnp.sum(gwd.astype(f32), axis=0, keepdims=True),
    )


def solution(mesh):
    lay = Layout(mesh.shape["dp"], mesh.shape["seq"])
    return jax.shard_map(
        functools.partial(body, lay),
        mesh=mesh,
        in_specs=(
            P(("dp", "seq"), None, None),
            P(("dp", "seq"), None),
            P(("dp", "seq"), None),
            P(("dp", "seq"), None),
            P(("dp", "seq")),
            P(("dp", "seq")),
            P("dp", "seq", None),
            P("dp", "seq", None),
            P("dp", None),
            P(("dp", "seq"), None, None),
            P(("dp", "seq"), None, None),
            P(("dp", "seq"), None, None),
        ),
        out_specs=(
            P(("dp", "seq"), None, None),
            P(("dp", "seq"), None, None),
            P(("dp", "seq"), None),
            P(("dp", "seq"), None),
            P(("dp", "seq"), None),
            P(("dp", "seq")),
            P(("dp", "seq")),
            P("dp", "seq", None),
            P("dp", "seq", None),
        ),
        check_vma=False,
    )
```

```python
import functools

import jax
import jax.numpy as jnp
from jax import lax
from jax.experimental import pallas as pl
from jax.experimental.pallas import tpu as pltpu
from jax.sharding import PartitionSpec as P

HEADS = 8
EPSILON = 1e-06
NEGATIVE = -1e30
MESH = pl.DeviceIdType.MESH
bf16, f32 = jnp.bfloat16, jnp.float32
NN = (((1,), (0,)), ((), ()))
NT = (((1,), (1,)), ((), ()))
TN = (((0,), (0,)), ((), ()))
LANES = 128
GAIN_LANE = 64
VMEM_LIMIT = 60 << 20
Shape = jax.ShapeDtypeStruct


def dot(a, b, dims=NN):
    return lax.dot_general(a, b, dims, preferred_element_type=f32)


def pad_rows(values, rows):
    extra = rows - values.shape[0]
    if extra == 0:
        return values
    return jnp.concatenate([values, jnp.zeros((extra, values.shape[1]), values.dtype)], axis=0)


def norm_rows(values):
    centred = values - jnp.mean(values, axis=-1, keepdims=True)
    inverse = lax.rsqrt(jnp.mean(centred * centred, axis=-1, keepdims=True) + EPSILON)
    return centred * inverse, inverse


def norm_back(grad_hat, normed, inverse):
    return inverse * (
        grad_hat
        - jnp.mean(grad_hat, axis=-1, keepdims=True)
        - normed * jnp.mean(grad_hat * normed, axis=-1, keepdims=True)
    )


def router_softmax(logits, experts):
    lane = lax.broadcasted_iota(jnp.int32, logits.shape, 1)
    logits = jnp.where(lane < experts, logits, NEGATIVE)
    exps = jnp.exp(logits - jnp.max(logits, axis=1, keepdims=True))
    return exps / jnp.sum(exps, axis=1, keepdims=True)


def gelu_parts(inner):
    k, c = 0.7978845608028654, 0.044715
    square = inner * inner
    t = jnp.tanh(inner * (k + (k * c) * square))
    half = 0.5 + 0.5 * t
    value = inner * half
    slope = half + value * (1.0 - half) * (2 * k + (6 * k * c) * square)
    return value, slope


def anywhere():
    return pl.BlockSpec(memory_space=pl.ANY)


def per_image(*dims):
    return pl.BlockSpec((1,) + dims, lambda i: (i,) + (0,) * len(dims))


def fixed(*dims):
    return pl.BlockSpec(dims, lambda i: (0,) * len(dims), pipeline_mode=pl.Buffered(1))


class Layout:
    def __init__(self, dp, seq):
        self.N, self.S = dp, seq
        self.L = dp // seq

    def here(self):
        dp, s = lax.axis_index("dp"), lax.axis_index("seq")
        return dp, s, dp // self.L, lax.rem(dp, self.L)

    def member_device(self, g, m):
        return (g * self.L + m // self.S, lax.rem(m, self.S))

    def group_peers(self):
        _, s, g, l = self.here()
        return [self.member_device(g, jnp.bitwise_xor(l * self.S + s, k)) for k in range(1, self.N)]

    def weight_peers(self):
        _, s, g, l = self.here()
        count = self.S * self.S
        places = [lax.rem(g * self.S + s + i, count) for i in range(1, count)]
        return [(q // self.S * self.L + l, lax.rem(q, self.S)) for q in places]

    def order(self):
        bits = [1 << i for i in range(self.N.bit_length() - 1) if 1 << i != self.S]
        left, loads, picked = list(range(1, self.N)), [0] * len(bits), []

        def after(k):
            return [load + (k & bit > 0) for load, bit in zip(loads, bits)]

        while left:
            k = min(left, key=lambda k: (max(after(k)) - min(after(k)), -sum(after(k)), k))
            left.remove(k)
            picked.append(k)
            loads = after(k)
        return picked

    def nth(self, i):
        k = jnp.int32(0)
        for n, value in enumerate(self.order()):
            k = jnp.where(i == n + 1, value, k)
        return k

    def expert_of(self, g, m):
        l, s = m // self.S, lax.rem(m, self.S)
        return lax.rem(g + s + l, self.S) * self.L + l


def greet(peers):
    barrier = pltpu.get_barrier_semaphore()
    for peer in peers:
        pl.semaphore_signal(barrier, inc=1, device_id=peer, device_id_type=MESH)
    pl.semaphore_wait(barrier, len(peers))


class Rows:
    def __init__(self, dp, seq):
        self.A, self.S = dp // 4, seq

    def here(self):
        dp, s = lax.axis_index("dp"), lax.axis_index("seq")
        return dp // 4, lax.rem(dp // 2, 2), lax.rem(dp, 2), s

    def device(self, a, b, c, s):
        return ((a * 2 + b) * 2 + c, s)

    def along_a(self):
        a, b, c, s = self.here()
        return [(i, lax.rem(a + i, self.A)) for i in range(1, self.A)]

    def plane(self):
        a, b, c, s = self.here()
        for i in range(1, 2 * self.S):
            if self.S == 1:
                yield i, 1 - b, s, 0
            else:
                q = lax.rem(b * self.S + s + i, 2 * self.S)
                yield i, q // self.S, lax.rem(q, self.S), lax.rem(q, self.S)


def attend(heads, qkv, keep, width):
    head = width // heads
    outs, lses = [], []
    for h in range(heads):
        q = qkv[:, h * head : (h + 1) * head]
        k = qkv[:, width + h * head : width + (h + 1) * head]
        v = qkv[:, 2 * width + h * head : 2 * width + (h + 1) * head]
        scores = jnp.where(keep, dot(q, k, NT) * (head**-0.5), NEGATIVE)
        row_max = jnp.max(scores, axis=1, keepdims=True)
        exps = jnp.exp(scores - row_max)
        totals = jnp.sum(exps, axis=1, keepdims=True)
        lses.append(row_max + jnp.log(totals))
        outs.append(dot((exps / totals).astype(bf16), v).astype(bf16))
    return jnp.concatenate(outs, axis=1), jnp.concatenate(lses, axis=1)


def front_kernel(
    lay, rows, experts,
    own_refs, tok_ref, mask_ref, cot_ref, code_ref, w_in_ref, w_down_ref,
    pack_ref, gains_ref, qkv_ref, att_ref, res_ref, lse_ref, routed_ref, probs_ref,
    gx_ref, zy_ref, gate_ref, gwi_ref, gwd_ref,
    own, full, routed, cot, w_in, w_down, x_send, c_send, x_recv, c_recv, gate_send, gwi, gwd,
    ps, pr, ws, wr, xs, xr, cs, cr, gs, gr, ts, tr, zs, ls,
):
    step = pl.program_id(0)
    steps = pl.num_programs(0)
    a, b, c, s = rows.here()
    _, _, g, l = lay.here()
    S, L = lay.S, lay.L
    members, cap, width = x_send.shape
    images, height = routed.shape[0], routed.shape[1]
    me = l * S + s
    delta = lax.rem(s + l, S)
    part_rows = w_in.shape[0] // S
    piece_rows = max(part_rows // 8, 16)

    def remote(src, dst, send, recv, device):
        return pltpu.make_async_remote_copy(src, dst, send, recv, device_id=device, device_id_type=MESH)

    def to_member(src, dst, send, recv, k):
        return remote(src, dst, send.at[k], recv.at[k], lay.member_device(g, jnp.bitwise_xor(me, k)))

    def x_copy(k):
        return to_member(x_send.at[jnp.bitwise_xor(me, k)], x_recv.at[me], xs, xr, k)

    def c_copy(k):
        return to_member(c_send.at[jnp.bitwise_xor(me, k)], c_recv.at[me], cs, cr, k)

    def gx_copy(k):
        return to_member(c_send.at[jnp.bitwise_xor(me, k)], gx_ref.at[me], gs, gr, k)

    def gate_copy(k):
        return to_member(gate_send.at[jnp.bitwise_xor(me, k)], gate_ref.at[me], ts, tr, k)

    def zy_copy(k):
        m = jnp.bitwise_xor(me, k)
        return pltpu.make_async_copy(x_send.at[m], zy_ref.at[m], zs.at[k])

    def pick_rows(m, values, target):
        slot = lax.broadcasted_iota(jnp.int32, (cap, images * height), 0) + m * cap
        hit = (code_ref[0:1, :] == slot) | (code_ref[1:2, :] == slot)
        pick = jnp.where(hit, 1.0, 0.0).astype(bf16)
        target[m] = dot(pick, values[...].reshape(images * height, width)).astype(bf16)

    def build_c(first, last):
        def build(i, carry):
            pick_rows(jnp.bitwise_xor(me, lay.nth(i + 1)), cot, c_send)
            return carry

        lax.fori_loop(first, last, build, 0)

    def weight_copies(d, first=0, count=part_rows):
        device = (lax.rem(g - d + S, S) * L + l, lax.rem(d - l + L * S, S))
        there = pl.ds(pl.multiple_of(s * part_rows + first, 16), count)
        return [
            remote(src.at[0, pl.ds(first, count)], dst.at[there], ws.at[2 * d + i], wr.at[2 * s + i], device)
            for i, (src, dst) in enumerate(((w_in_ref, w_in), (w_down_ref, w_down)))
        ]

    def weight_pieces(d, q):
        for copy in weight_copies(d, q * piece_rows, piece_rows):
            copy.start()

    def weight_local():
        mine = pl.ds(pl.multiple_of(s * part_rows, part_rows), part_rows)
        return [
            pltpu.make_async_copy(src.at[0], dst.at[mine], wr.at[2 * s + i])
            for i, (src, dst) in enumerate(((w_in_ref, w_in), (w_down_ref, w_down)))
        ]

    @pl.when(step == 0)
    def _():
        greet(
            [rows.device(i, b, c, s) for _, i in rows.along_a()]
            + [rows.device(a, b2, c, s2) for _, b2, s2, _ in rows.plane()]
            + [rows.device(a, b, 1 - c, s)]
            + lay.group_peers()
            + lay.weight_peers()
        )
        A, Q = rows.A, 2 * rows.S
        sl = s if rows.S > 1 else 0
        first = 0
        for ref in own_refs:
            own[:, first : first + ref.shape[1]] = ref[...]
            first += ref.shape[1]
        third = members // 3
        order = lay.order()
        pieces = part_rows // piece_rows
        todo = [(q, d) for q in range(pieces) for d in (*range(1, S), 0)]

        def send(first, last):
            for n in range(first, last):
                c_copy(order[n]).start()
                for q, d in todo[n * len(todo) // len(order) : (n + 1) * len(todo) // len(order)]:
                    if d:
                        weight_pieces(d, q)
                    else:

                        @pl.when(delta != 0)
                        def _():
                            weight_pieces(0, q)

        local = pltpu.make_async_copy(own, full.at[a, b, c, sl], ls.at[0])
        local.start()
        copies = [
            remote(own, full.at[a, b, c, sl], ps.at[i], pr.at[i], rows.device(a2, b, c, s))
            for i, a2 in rows.along_a()
        ]
        for copy in copies:
            copy.start()
        for i in range(images):
            cot[i] = pad_rows(cot_ref[i].astype(f32), height).astype(bf16)
        build_c(0, third)
        local.wait()
        for copy in copies:
            copy.wait()
        copies = [
            remote(
                full.at[:, b, c, sl], full.at[:, b, c, sl], ps.at[A + i], pr.at[A + i], rows.device(a, b2, c, s2)
            )
            for i, b2, s2, _ in rows.plane()
        ]
        for copy in copies:
            copy.start()
        build_c(third, members)
        for copy in copies:
            copy.wait()
        last = remote(
            full.at[:, :, c], full.at[:, :, c], ps.at[A + Q], pr.at[A + Q], rows.device(a, b, 1 - c, s)
        )
        last.start()

        @pl.when(delta == 0)
        def _():
            for copy in weight_local():
                copy.start()

        send(0, members - 1)
        c_recv[me] = c_send[me]
        last.wait()
        pack_ref[...] = full[...].reshape(pack_ref.shape)
        tail = pack_ref[:, 4 * width :].astype(f32).T
        gains_ref[...] = tail[GAIN_LANE : GAIN_LANE + 8, :]

    inputs = pad_rows(tok_ref[0].astype(f32), height)
    hat, _ = norm_rows(inputs)
    normed = (hat * gains_ref[0:1, :]).astype(bf16)
    qkv = dot(normed, pack_ref[:, 0 : 3 * width]).astype(bf16)
    qkv_ref[0] = qkv
    att, lse = attend(HEADS, qkv, mask_ref[0] > 0, width)
    att_ref[0] = att
    lse_ref[0] = lse
    residual = inputs + dot(att, pack_ref[:, 3 * width : 4 * width])
    res_ref[0] = residual
    hat, _ = norm_rows(residual)
    routed_now = (hat * gains_ref[1:2, :]).astype(bf16)
    routed_ref[0] = routed_now
    routed[step] = routed_now
    probs_ref[0] = router_softmax(dot(routed_now, pack_ref[:, 4 * width :]), experts)

    @pl.when(step == steps - 1)
    def _():
        def dispatch(i, carry):
            k = lay.nth(i)
            pick_rows(jnp.bitwise_xor(me, k), routed, x_send)
            x_copy(k).start()
            return carry

        lax.fori_loop(1, members, dispatch, 0)
        pick_rows(me, routed, x_send)
        x_recv[me] = x_send[me]
        gwi[...] = jnp.zeros_like(gwi)
        gwd[...] = jnp.zeros_like(gwd)

        for p in range(S):
            for copy_in in range(2):
                span = pl.ds(p * part_rows, part_rows)
                dst = (w_in, w_down)[copy_in].at[span]
                src = (w_in_ref, w_down_ref)[copy_in].at[0]

                @pl.when((delta == 0) & (s == p))
                def _():
                    pltpu.make_async_copy(src, dst, wr.at[2 * p + copy_in]).wait()

                @pl.when((delta != 0) | (s != p))
                def _():
                    remote(src, dst, ws.at[0], wr.at[2 * p + copy_in], (0, 0)).wait_recv()

        mine = lay.expert_of(g, me)
        hidden = w_in.shape[1]
        chunk = min(512, hidden)

        def work(j, carry):
            ks = (lay.nth(2 * j), lay.nth(2 * j + 1))
            ms = [jnp.bitwise_xor(me, k) for k in ks]

            @pl.when(j > 0)
            def _():
                x_copy(ks[0]).wait()
                c_copy(ks[0]).wait()

            x_copy(ks[1]).wait()
            c_copy(ks[1]).wait()
            x = jnp.concatenate([x_recv[m] for m in ms], axis=0)
            cf = jnp.concatenate([c_recv[m] for m in ms], axis=0).astype(f32)
            probs = router_softmax(dot(x, pack_ref[:, 4 * width :]), experts)
            lane = lax.broadcasted_iota(jnp.int32, probs.shape, 1)
            gate = jnp.sum(jnp.where(lane == mine, probs, 0.0), axis=1, keepdims=True)
            dy = (gate * cf).astype(bf16)
            y, gx = None, None
            for f in range(0, hidden, chunk):
                span = slice(f, f + chunk)
                value, slope = gelu_parts(dot(x, w_in[:, span]))
                act = value.astype(bf16)
                inner_grad = (dot(dy, w_down[:, span]) * slope).astype(bf16)
                y_part, gx_part = dot(act, w_down[:, span], NT), dot(inner_grad, w_in[:, span], NT)
                y = y_part if y is None else y + y_part
                gx = gx_part if gx is None else gx + gx_part
                gwd[:, span] += dot(dy, act, TN)
                gwi[:, span] += dot(x, inner_grad, TN)
            zy = (gate * y).astype(bf16)
            gxb = gx.astype(bf16)
            gate_grad = jnp.broadcast_to(jnp.sum(y * cf, axis=1, keepdims=True), (2 * cap, LANES)).T
            for q in range(2):
                c_send[ms[q]] = gxb[q * cap : (q + 1) * cap]
                x_send[ms[q]] = zy[q * cap : (q + 1) * cap]
                gate_send[ms[q]] = gate_grad[0:8, q * cap : (q + 1) * cap]

            @pl.when(j > 0)
            def _():
                gx_copy(ks[0]).start()
                gate_copy(ks[0]).start()

            gx_copy(ks[1]).start()
            gate_copy(ks[1]).start()
            zy_copy(ks[0]).start()
            zy_copy(ks[1]).start()
            return carry

        lax.fori_loop(0, members // 2, work, 0)
        keeps = [
            pltpu.make_async_copy(c_send.at[me], gx_ref.at[me], ls.at[0]),
            pltpu.make_async_copy(gate_send.at[me], gate_ref.at[me], ls.at[1]),
        ]
        for keep in keeps:
            keep.start()
        gwi_ref[...] = gwi[...].astype(bf16)
        gwd_ref[...] = gwd[...].astype(bf16)
        for keep in keeps:
            keep.wait()
        zy_copy(0).wait()
        for d in range(1, S):
            for copy in weight_copies(d):
                copy.wait_send()

        @pl.when(delta != 0)
        def _():
            for copy in weight_copies(0):
                copy.wait_send()

        def finish(k, carry):
            gx_copy(k).wait()
            gate_copy(k).wait()
            zy_copy(k).wait()
            return carry

        lax.fori_loop(1, members, finish, 0)


def front(lay, rows, experts, cap, own, tokens, mask, cotangent, codes, w_in, w_down):
    S, M = lay.S, lay.N
    images, positions, width = tokens.shape
    height = mask.shape[2]
    hidden = w_in.shape[-1]
    blocks = (M, cap, width)
    own_shape = (own[0].shape[0], sum(part.shape[1] for part in own))
    full = (rows.A, 2, 2, rows.S) + own_shape
    total = rows.A * 4 * rows.S * own_shape[0]
    dma = lambda n: pltpu.SemaphoreType.DMA((n,))
    count = rows.A + 2 * rows.S + 1
    return pl.pallas_call(
        functools.partial(front_kernel, lay, rows, experts),
        grid=(images,),
        out_shape=(
            Shape((total, own_shape[1]), bf16),
            Shape((8, width), f32),
            Shape((images, height, 3 * width), bf16),
            Shape((images, height, width), bf16),
            Shape((images, height, width), f32),
            Shape((images, height, HEADS), f32),
            Shape((images, height, width), bf16),
            Shape((images, height, LANES), f32),
            Shape(blocks, bf16),
            Shape(blocks, bf16),
            Shape((M, 8, cap), f32),
            Shape((width, hidden), bf16),
            Shape((width, hidden), bf16),
        ),
        in_specs=[
            [fixed(*part.shape) for part in own],
            per_image(positions, width),
            per_image(1, height),
            fixed(*cotangent.shape),
            fixed(*codes.shape),
            anywhere(),
            anywhere(),
        ],
        out_specs=(
            fixed(total, own_shape[1]),
            fixed(8, width),
            per_image(height, 3 * width),
            per_image(height, width),
            per_image(height, width),
            per_image(height, HEADS),
            per_image(height, width),
            per_image(height, LANES),
            anywhere(),
            anywhere(),
            anywhere(),
            fixed(width, hidden),
            fixed(width, hidden),
        ),
        scratch_shapes=[
            pltpu.VMEM(own_shape, bf16),
            pltpu.VMEM(full, bf16),
            pltpu.VMEM((images, height, width), bf16),
            pltpu.VMEM((images, height, width), bf16),
            pltpu.VMEM((width, hidden), bf16),
            pltpu.VMEM((width, hidden), bf16),
            *[pltpu.VMEM(blocks, bf16)] * 4,
            pltpu.VMEM((M, 8, cap), f32),
            pltpu.VMEM((width, hidden), f32),
            pltpu.VMEM((width, hidden), f32),
            dma(count), dma(count), dma(2 * S), dma(2 * S),
            *[dma(M)] * 9,
            dma(2),
        ],
        compiler_params=pltpu.CompilerParams(
            collective_id=0, has_side_effects=True, vmem_limit_bytes=VMEM_LIMIT, dimension_semantics=("arbitrary",)
        ),
    )(own, tokens, mask, cotangent, codes, w_in, w_down)


def back_kernel(
    lay, rows,
    tok_ref, mask_ref, cot_ref, code_ref, qkv_ref, att_ref, res_ref, lse_ref, routed_ref, probs_ref,
    pack_ref, gains_ref, gx_ref, gate_ref, zy_ref, gwi_ref, gwd_ref,
    gtok_ref, mixed_ref, own_ref, gwi_parts, gwd_parts,
    gqkv, gout, grest, table, ggain, residuals, codes, zy, part, recv1, sum1, recv2, sum2, recv3,
    ps, pr, zs, zr, ws, wr, ls,
):
    step = pl.program_id(0)
    images = pl.num_programs(0)
    a, b, c, s = rows.here()
    _, _, g, l = lay.here()
    S, L = lay.S, lay.L
    me = l * S + s
    delta = lax.rem(s + l, S)
    members, _, cap = gate_ref.shape
    slots = members * cap
    height, width = att_ref.shape[1], att_ref.shape[2]
    positions = gtok_ref.shape[1]
    head = width // HEADS
    part_rows = gwi_ref.shape[0] // S
    piece_rows = max(part_rows // 8, 16)

    def remote(src, dst, send, recv, device):
        return pltpu.make_async_remote_copy(src, dst, send, recv, device_id=device, device_id_type=MESH)

    def zy_copy(k):
        m = jnp.bitwise_xor(me, k)
        return remote(zy_ref.at[m], zy.at[me], zs.at[k], zr.at[k], lay.member_device(g, m))

    owner = lax.rem(g + delta, S)

    def weight_pairs(p, first=0, count=part_rows):
        span, there = pl.ds(p * part_rows + first, count), pl.ds(first, count)
        return ((gwi_ref.at[span], gwi_parts.at[g, there]), (gwd_ref.at[span], gwd_parts.at[g, there]))

    def weight_copies(p, first=0, count=part_rows):
        return [
            remote(src, dst, ws.at[2 * p + i], wr.at[2 * g + i], (owner * L + l, p))
            for i, (src, dst) in enumerate(weight_pairs(p, first, count))
        ]

    def weight_local(p):
        return [
            pltpu.make_async_copy(src, dst, ws.at[2 * p + i]) for i, (src, dst) in enumerate(weight_pairs(p))
        ]

    def weight_pieces(p, q):
        @pl.when((delta != 0) | (s != p))
        def _():
            for copy in weight_copies(p, q * piece_rows, piece_rows):
                copy.start()

    zy_keep = pltpu.make_async_copy(zy_ref.at[me], zy.at[me], ls.at[0])

    @pl.when(step == 0)
    def _():
        greet(
            [rows.device(i, b, c, s) for _, i in rows.along_a()]
            + [rows.device(a, b2, c, s2) for _, b2, s2, _ in rows.plane()]
            + [rows.device(a, b, 1 - c, s)]
            + lay.group_peers()
            + lay.weight_peers()
        )
        pieces = part_rows // piece_rows
        todo = [(p, q) for q in range(pieces) for p in range(S)]
        order = lay.order()
        for n, k in enumerate(order):
            for p, q in todo[n * len(todo) // len(order) : (n + 1) * len(todo) // len(order)]:
                weight_pieces(p, q)
            zy_copy(k).start()
        zy_keep.start()
        for p in range(S):

            @pl.when((delta == 0) & (s == p))
            def _():
                for copy in weight_local(p):
                    copy.start()

        for ref in (gqkv, gout, grest, ggain):
            ref[...] = jnp.zeros_like(ref)
        for m in range(members):
            values = gate_ref[m].T[:, 0:1]
            high = values.astype(bf16).astype(f32)
            lane = lax.broadcasted_iota(jnp.int32, (cap, LANES), 1)
            here = lane == lay.expert_of(g, jnp.int32(m))
            span = slice(m * cap, (m + 1) * cap)
            table[span, 0:LANES] = jnp.where(here, high, 0.0).astype(bf16)
            table[span, LANES : 2 * LANES] = jnp.where(here, values - high, 0.0).astype(bf16)

    def pick_slots(code):
        slot = lax.broadcasted_iota(jnp.int32, (height, slots), 1)
        return jnp.where((code[:, 0:1] == slot) | (code[:, 1:2] == slot), 1.0, 0.0).astype(bf16)

    wide = jnp.concatenate([code_ref[0].astype(f32), jnp.zeros((6, height), f32)], axis=0)
    codes[step] = wide.T.astype(jnp.int32)
    residuals[step] = res_ref[0]
    pick = pick_slots(codes[step])
    grad_routed = dot(pick, gx_ref[...].reshape(slots, width))
    both = dot(pick, table[...])
    grad_probs = both[:, :LANES] + both[:, LANES:]
    probs = probs_ref[0]
    grad_logits = probs * (grad_probs - jnp.sum(grad_probs * probs, axis=1, keepdims=True))
    logit_high = grad_logits.astype(bf16)
    logit_low = (grad_logits - logit_high.astype(f32)).astype(bf16)
    router = pack_ref[:, 4 * width :]
    grad_router = dot(routed_ref[0], jnp.concatenate([logit_high, logit_low], axis=1), TN)
    grest[...] += grad_router[:, :LANES] + grad_router[:, LANES:]
    grad_routed += dot(logit_high, router, NT) + dot(logit_low, router, NT)
    hat_two, inverse_two = norm_rows(res_ref[0])
    ggain[1:2, :] += jnp.sum(grad_routed * hat_two, axis=0, keepdims=True)
    grad_residual = pad_rows(cot_ref[0].astype(f32), height) + norm_back(
        grad_routed * gains_ref[1:2, :], hat_two, inverse_two
    )
    grad_att = grad_residual.astype(bf16)
    gout[...] += dot(att_ref[0], grad_att, TN)
    grad_attended = dot(grad_att, pack_ref[:, 3 * width : 4 * width], NT).astype(bf16)
    keep = mask_ref[0] > 0
    qkv, lse = qkv_ref[0], lse_ref[0]
    scale = head**-0.5
    grad_q, grad_k, grad_v = [], [], []
    for h in range(HEADS):
        q = qkv[:, h * head : (h + 1) * head]
        k = qkv[:, width + h * head : width + (h + 1) * head]
        v = qkv[:, 2 * width + h * head : 2 * width + (h + 1) * head]
        ga = grad_attended[:, h * head : (h + 1) * head]
        scores = jnp.where(keep, dot(q, k, NT) * scale, NEGATIVE)
        weights = jnp.exp(scores - lse[:, h : h + 1])
        grad_v.append(dot(weights.astype(bf16), ga, TN).astype(bf16))
        grad_weights = dot(ga, v, NT)
        row = jnp.sum(weights * grad_weights, axis=1, keepdims=True)
        grad_scores = (weights * (grad_weights - row)).astype(bf16)
        grad_q.append((dot(grad_scores, k) * scale).astype(bf16))
        grad_k.append((dot(grad_scores, q, TN) * scale).astype(bf16))
    grad_qkv = jnp.concatenate(grad_q + grad_k + grad_v, axis=1)
    hat_one, inverse_one = norm_rows(pad_rows(tok_ref[0].astype(f32), height))
    normed = (hat_one * gains_ref[0:1, :]).astype(bf16)
    gqkv[...] += dot(normed, grad_qkv, TN)
    grad_normed = dot(grad_qkv, pack_ref[:, 0 : 3 * width], NT)
    ggain[0:1, :] += jnp.sum(grad_normed * hat_one, axis=0, keepdims=True)
    grad_inputs = grad_residual + norm_back(grad_normed * gains_ref[0:1, :], hat_one, inverse_one)
    gtok_ref[0] = grad_inputs[:positions]

    @pl.when(step == images - 1)
    def _():
        A, Q = rows.A, 2 * rows.S
        zeros = jnp.zeros((GAIN_LANE, width), f32)
        tail = jnp.concatenate([zeros, ggain[...], zeros[: GAIN_LANE - 8]], axis=0)
        grest[...] += tail.T
        shape = part.shape[:5]
        part[..., 0 : 3 * width] = gqkv[...].astype(bf16).reshape(shape + (3 * width,))
        part[..., 3 * width : 4 * width] = gout[...].astype(bf16).reshape(shape + (width,))
        part[..., 4 * width :] = grest[...].astype(bf16).reshape(shape + (LANES,))
        first = remote(part.at[:, :, 1 - c], recv1, ps.at[0], pr.at[0], rows.device(a, b, 1 - c, s))
        first.start()

        def wait_zy(k, carry):
            zy_copy(k).wait()
            return carry

        lax.fori_loop(1, members, wait_zy, 0)
        zy_keep.wait()

        def mix(first_image, last_image):
            def one(i, carry):
                mixed = residuals[i] + dot(pick_slots(codes[i]), zy[...].reshape(slots, width))
                mixed_ref[i] = mixed[:positions].astype(bf16)
                return carry

            lax.fori_loop(first_image, last_image, one, 0)

        count = residuals.shape[0]
        mix(0, count // 4)
        first.wait()
        sum1[...] = (part[:, :, c].astype(f32) + recv1[...].astype(f32)).astype(bf16)
        copies = [
            remote(sum1.at[:, b2, sl2], recv2.at[i - 1], ps.at[i], pr.at[i], rows.device(a, b2, c, s2))
            for i, b2, s2, sl2 in rows.plane()
        ]
        for copy in copies:
            copy.start()
        mix(count // 4, count * 3 // 4)
        for copy in copies:
            copy.wait()
        sl = s if rows.S > 1 else 0
        total = sum1[:, b, sl].astype(f32)
        for i in range(Q - 1):
            total += recv2[i].astype(f32)
        sum2[...] = total.astype(bf16)
        copies = [
            remote(sum2.at[a2], recv3.at[i - 1], ps.at[Q + i], pr.at[Q + i], rows.device(a2, b, c, s))
            for i, a2 in rows.along_a()
        ]
        for copy in copies:
            copy.start()
        mix(count * 3 // 4, count)
        for copy in copies:
            copy.wait()
        final = sum2[a].astype(f32)
        for i in range(A - 1):
            final += recv3[i].astype(f32)
        own_ref[...] = final

        for p in range(S):

            @pl.when((delta == 0) & (s == p))
            def _():
                for copy in weight_local(p):
                    copy.wait()

            @pl.when((delta != 0) | (s != p))
            def _():
                for copy in weight_copies(p):
                    copy.wait_send()

        for q in range(S):
            @pl.when((delta != 0) | (g != q))
            def _():
                for i, (src, dst) in enumerate(((gwi_ref, gwi_parts), (gwd_ref, gwd_parts))):
                    span = pl.ds(0, part_rows)
                    remote(src.at[span], dst.at[q], ws.at[i], wr.at[2 * q + i], (0, 0)).wait_recv()


def back(
    lay, rows, own_height, tokens, mask, cotangent, code, qkv, att, res, lse, routed, probs, pack, gains, gx, gate,
    zy, gwi, gwd,
):
    images, positions, width = tokens.shape
    height = att.shape[1]
    M, _, cap = gate.shape
    slots = M * cap
    A, S = rows.A, rows.S
    G = lay.S
    hidden = gwi.shape[1]
    part_rows = gwi.shape[0] // G
    columns = pack.shape[1]
    dma = lambda n: pltpu.SemaphoreType.DMA((n,))
    count = A + 2 * S + 1
    return pl.pallas_call(
        functools.partial(back_kernel, lay, rows),
        grid=(images,),
        out_shape=(
            Shape((images, positions, width), f32),
            Shape((images, positions, width), bf16),
            Shape((own_height, columns), f32),
            Shape((G, part_rows, hidden), bf16),
            Shape((G, part_rows, hidden), bf16),
        ),
        in_specs=[
            per_image(positions, width),
            per_image(1, height),
            per_image(positions, width),
            per_image(2, height),
            per_image(height, 3 * width),
            per_image(height, width),
            per_image(height, width),
            per_image(height, HEADS),
            per_image(height, width),
            per_image(height, LANES),
            fixed(*pack.shape),
            fixed(*gains.shape),
            fixed(*gx.shape),
            fixed(*gate.shape),
            anywhere(),
            anywhere(),
            anywhere(),
        ],
        out_specs=(
            per_image(positions, width),
            fixed(images, positions, width),
            fixed(own_height, columns),
            anywhere(),
            anywhere(),
        ),
        scratch_shapes=[
            pltpu.VMEM((width, 3 * width), f32),
            pltpu.VMEM((width, width), f32),
            pltpu.VMEM((width, LANES), f32),
            pltpu.VMEM((slots, 2 * LANES), bf16),
            pltpu.VMEM((8, width), f32),
            pltpu.VMEM((images, height, width), f32),
            pltpu.VMEM((images, height, 8), jnp.int32),
            pltpu.VMEM((M, cap, width), bf16),
            pltpu.VMEM((A, 2, 2, S, own_height, columns), bf16),
            pltpu.VMEM((A, 2, S, own_height, columns), bf16),
            pltpu.VMEM((A, 2, S, own_height, columns), bf16),
            pltpu.VMEM((2 * S - 1, A, own_height, columns), bf16),
            pltpu.VMEM((A, own_height, columns), bf16),
            pltpu.VMEM((A - 1, own_height, columns), bf16),
            dma(count), dma(count), dma(M), dma(M), dma(2 * G), dma(2 * G), dma(1),
        ],
        compiler_params=pltpu.CompilerParams(
            collective_id=1, has_side_effects=True, vmem_limit_bytes=VMEM_LIMIT, dimension_semantics=("arbitrary",)
        ),
    )(tokens, mask, cotangent, code, qkv, att, res, lse, routed, probs, pack, gains, gx, gate, zy, gwi, gwd)


def finish_kernel(sums_ref, gwi_parts, gwd_parts, qkv_ref, out_ref, router_ref, gain_one, gain_two, gwi_ref, gwd_ref):
    width = out_ref.shape[1]
    step = pl.program_id(0)

    @pl.when(step == 0)
    def _():
        qkv_ref[...] = sums_ref[:, : 3 * width]
        out_ref[...] = sums_ref[:, 3 * width : 4 * width]
        rest = sums_ref[:, 4 * width :]
        router_ref[...] = rest[:, : router_ref.shape[1]]
        height = rest.shape[0]
        tall = pad_rows(rest, max(height, 8)).T
        gain_one[...] = tall[GAIN_LANE : GAIN_LANE + 1, :height]
        gain_two[...] = tall[GAIN_LANE + 1 : GAIN_LANE + 2, :height]

    for parts, ref in ((gwi_parts, gwi_ref), (gwd_parts, gwd_ref)):
        total = parts[0].astype(f32)
        for q in range(1, parts.shape[0]):
            total += parts[q].astype(f32)
        ref[0] = total


def finish(experts, width, sums, gwi, gwd):
    groups, part_rows, hidden = gwi.shape
    height = sums.shape[0]
    steps = 4 if part_rows % 64 == 0 else 1
    piece = part_rows // steps
    parts = pl.BlockSpec((groups, piece, hidden), lambda i: (0, i, 0))
    whole = pl.BlockSpec((1, piece, hidden), lambda i: (0, i, 0))
    qkv, out, router, gain_one, gain_two, gwi, gwd = pl.pallas_call(
        finish_kernel,
        grid=(steps,),
        out_shape=(
            Shape((height, 3 * width), f32),
            Shape((height, width), f32),
            Shape((height, experts), f32),
            Shape((1, height), f32),
            Shape((1, height), f32),
            Shape((1, part_rows, hidden), f32),
            Shape((1, part_rows, hidden), f32),
        ),
        in_specs=[fixed(*sums.shape), parts, parts],
        out_specs=(
            fixed(height, 3 * width),
            fixed(height, width),
            fixed(height, experts),
            fixed(1, height),
            fixed(1, height),
            whole,
            whole,
        ),
        compiler_params=pltpu.CompilerParams(vmem_limit_bytes=VMEM_LIMIT),
    )(sums, gwi, gwd)
    return qkv, out, router, gain_one.reshape(height), gain_two.reshape(height), gwi, gwd


def body(
    lay, tokens, w_qkv, w_attn_out, w_router, gain_attn, gain_moe, w_expert_in, w_expert_down, key_mask,
    expert_choice, slot_index, cotangent,
):
    images, positions, width = tokens.shape
    N, S, L = lay.N, lay.S, lay.L
    experts = w_router.shape[1]
    height = -(-positions // 16) * 16
    token_rows = images * positions
    capacity = ((token_rows * 10 + 4 * experts - 1) // (4 * experts) + 7) // 8 * 8
    dp, s, g, l = lay.here()

    lane = jnp.arange(LANES, dtype=jnp.int32)[None, :]
    rest = jnp.pad(w_router, ((0, 0), (0, LANES - experts)))
    rest = jnp.where(lane == GAIN_LANE, gain_attn[:, None], jnp.where(lane == GAIN_LANE + 1, gain_moe[:, None], rest))
    own = [w_qkv, w_attn_out, rest]
    few = w_qkv.shape[0] % 16 != 0
    if few:
        own = [lax.all_gather(part, "seq", axis=0, tiled=True) for part in own]
    rows = Rows(N, 1 if few else S)

    mask = lax.dynamic_slice_in_dim(key_mask, s * images, images, axis=0)
    mask = jnp.pad(mask, ((0, 0), (0, height - positions)))[:, None, :]
    choice, slot = expert_choice.transpose(0, 2, 1), slot_index.transpose(0, 2, 1)
    group, local = choice // L, lax.rem(choice, L)
    member = local * S + lax.rem(group - g - local + (L + 1) * S, S)
    code = jnp.where(slot >= 0, member * capacity + slot, -1)
    code = jnp.pad(code, ((0, 0), (0, 0), (0, height - positions)), constant_values=-1)
    code_rows = code.transpose(1, 0, 2).reshape(2, images * height)

    pack, gains, qkv, att, res, lse, routed, probs, gx, zy, gate, gwi, gwd = front(
        lay, rows, experts, capacity, own, tokens, mask, cotangent, code_rows, w_expert_in, w_expert_down
    )
    gtok, mixed, sums, gwi, gwd = back(
        lay, rows, own[0].shape[0], tokens, mask, cotangent, code, qkv, att, res, lse, routed, probs, pack, gains, gx,
        gate, zy, gwi, gwd,
    )
    if few:
        sums = lax.psum_scatter(sums, "seq", scatter_dimension=0, tiled=True)
    return (mixed, gtok, *finish(experts, width, sums, gwi, gwd))


def solution(mesh):
    lay = Layout(mesh.shape["dp"], mesh.shape["seq"])
    return jax.shard_map(
        functools.partial(body, lay),
        mesh=mesh,
        in_specs=(
            P(("dp", "seq"), None, None),
            P(("dp", "seq"), None),
            P(("dp", "seq"), None),
            P(("dp", "seq"), None),
            P(("dp", "seq")),
            P(("dp", "seq")),
            P("dp", "seq", None),
            P("dp", "seq", None),
            P("dp", None),
            P(("dp", "seq"), None, None),
            P(("dp", "seq"), None, None),
            P(("dp", "seq"), None, None),
        ),
        out_specs=(
            P(("dp", "seq"), None, None),
            P(("dp", "seq"), None, None),
            P(("dp", "seq"), None),
            P(("dp", "seq"), None),
            P(("dp", "seq"), None),
            P(("dp", "seq")),
            P(("dp", "seq")),
            P("dp", "seq", None),
            P("dp", "seq", None),
        ),
        check_vma=False,
    )
```

```python
import functools

import jax
import jax.numpy as jnp
from jax import lax
from jax.experimental import pallas as pl
from jax.experimental.pallas import tpu as pltpu
from jax.sharding import PartitionSpec as P

HEADS = 8
EPSILON = 1e-06
NEGATIVE = -1e30
MESH = pl.DeviceIdType.MESH
bf16, f32 = jnp.bfloat16, jnp.float32
NN = (((1,), (0,)), ((), ()))
NT = (((1,), (1,)), ((), ()))
TN = (((0,), (0,)), ((), ()))
LANES = 128
GAIN_LANE = 64
LATE = 2
VMEM_LIMIT = 60 << 20
Shape = jax.ShapeDtypeStruct


def dot(a, b, dims=NN):
    return lax.dot_general(a, b, dims, preferred_element_type=f32)


def pad_rows(values, rows):
    extra = rows - values.shape[0]
    if extra == 0:
        return values
    return jnp.concatenate([values, jnp.zeros((extra, values.shape[1]), values.dtype)], axis=0)


def norm_rows(values):
    centred = values - jnp.mean(values, axis=-1, keepdims=True)
    inverse = lax.rsqrt(jnp.mean(centred * centred, axis=-1, keepdims=True) + EPSILON)
    return centred * inverse, inverse


def norm_back(grad_hat, normed, inverse):
    return inverse * (
        grad_hat
        - jnp.mean(grad_hat, axis=-1, keepdims=True)
        - normed * jnp.mean(grad_hat * normed, axis=-1, keepdims=True)
    )


def router_softmax(logits, experts):
    lane = lax.broadcasted_iota(jnp.int32, logits.shape, 1)
    logits = jnp.where(lane < experts, logits, NEGATIVE)
    exps = jnp.exp(logits - jnp.max(logits, axis=1, keepdims=True))
    return exps / jnp.sum(exps, axis=1, keepdims=True)


def gelu_parts(inner):
    k, c = 0.7978845608028654, 0.044715
    square = inner * inner
    t = jnp.tanh(inner * (k + (k * c) * square))
    half = 0.5 + 0.5 * t
    value = inner * half
    slope = half + value * (1.0 - half) * (2 * k + (6 * k * c) * square)
    return value, slope


def anywhere():
    return pl.BlockSpec(memory_space=pl.ANY)


def per_image(*dims):
    return pl.BlockSpec((1,) + dims, lambda i: (i,) + (0,) * len(dims))


def fixed(*dims):
    return pl.BlockSpec(dims, lambda i: (0,) * len(dims), pipeline_mode=pl.Buffered(1))


class Layout:
    def __init__(self, dp, seq):
        self.N, self.S = dp, seq
        self.L = dp // seq

    def here(self):
        dp, s = lax.axis_index("dp"), lax.axis_index("seq")
        return dp, s, dp // self.L, lax.rem(dp, self.L)

    def member_device(self, g, m):
        return (g * self.L + m // self.S, lax.rem(m, self.S))

    def group_peers(self):
        _, s, g, l = self.here()
        return [self.member_device(g, jnp.bitwise_xor(l * self.S + s, k)) for k in range(1, self.N)]

    def weight_peers(self):
        _, s, g, l = self.here()
        count = self.S * self.S
        places = [lax.rem(g * self.S + s + i, count) for i in range(1, count)]
        return [(q // self.S * self.L + l, lax.rem(q, self.S)) for q in places]

    def order(self):
        bits = [1 << i for i in range(self.N.bit_length() - 1) if 1 << i != self.S]
        left, loads, picked = list(range(1, self.N)), [0] * len(bits), []

        def after(k):
            return [load + (k & bit > 0) for load, bit in zip(loads, bits)]

        while left:
            k = min(left, key=lambda k: (max(after(k)) - min(after(k)), -sum(after(k)), k))
            left.remove(k)
            picked.append(k)
            loads = after(k)
        return picked

    def nth(self, i):
        k = jnp.int32(0)
        for n, value in enumerate(self.order()):
            k = jnp.where(i == n + 1, value, k)
        return k

    def expert_of(self, g, m):
        l, s = m // self.S, lax.rem(m, self.S)
        return lax.rem(g + s + l, self.S) * self.L + l


def greet(peers, meanwhile):
    barrier = pltpu.get_barrier_semaphore()
    for peer in peers:
        pl.semaphore_signal(barrier, inc=1, device_id=peer, device_id_type=MESH)
    meanwhile()
    pl.semaphore_wait(barrier, len(peers))


class Rows:
    def __init__(self, dp, seq):
        self.A, self.S = dp // 4, seq

    def here(self):
        dp, s = lax.axis_index("dp"), lax.axis_index("seq")
        return dp // 4, lax.rem(dp // 2, 2), lax.rem(dp, 2), s

    def device(self, a, b, c, s):
        return ((a * 2 + b) * 2 + c, s)

    def along_a(self):
        a, b, c, s = self.here()
        return [(i, lax.rem(a + i, self.A)) for i in range(1, self.A)]

    def plane(self):
        a, b, c, s = self.here()
        for i in range(1, 2 * self.S):
            if self.S == 1:
                yield i, 1 - b, s, 0
            else:
                q = lax.rem(b * self.S + s + i, 2 * self.S)
                yield i, q // self.S, lax.rem(q, self.S), lax.rem(q, self.S)


def attend(heads, qkv, keep, width, soft_ref):
    head = width // heads
    outs = []
    for h in range(heads):
        q = qkv[:, h * head : (h + 1) * head]
        k = qkv[:, width + h * head : width + (h + 1) * head]
        v = qkv[:, 2 * width + h * head : 2 * width + (h + 1) * head]
        scores = jnp.where(keep, dot(q, k, NT) * (head**-0.5), NEGATIVE)
        row_max = jnp.max(scores, axis=1, keepdims=True)
        exps = jnp.exp(scores - row_max)
        totals = jnp.sum(exps, axis=1, keepdims=True)
        soft = (exps / totals).astype(bf16)
        soft_ref[0, h] = soft
        outs.append(dot(soft, v).astype(bf16))
    return jnp.concatenate(outs, axis=1)


def front_kernel(
    lay, rows, experts,
    own_refs, tok_ref, mask_ref, cot_ref, code_ref, w_in_ref, w_down_ref,
    pack_ref, gains_ref, qkv_ref, att_ref, res_ref, soft_ref, routed_ref, probs_ref,
    gx_ref, zy_ref, gate_ref, gwi_ref, gwd_ref,
    own, full, routed, cot, w_in, w_down, x_send, c_send, x_recv, c_recv, gate_send, gwi, gwd,
    ps, pr, ws, wr, xs, xr, cs, cr, gs, gr, ts, tr, zs, ls,
):
    step = pl.program_id(0)
    steps = pl.num_programs(0)
    a, b, c, s = rows.here()
    _, _, g, l = lay.here()
    S, L = lay.S, lay.L
    members, cap, width = x_send.shape
    images, height = routed.shape[0], routed.shape[1]
    me = l * S + s
    delta = lax.rem(s + l, S)
    part_rows = w_in.shape[0] // S
    piece_rows = max(part_rows // 8, 16)

    def remote(src, dst, send, recv, device):
        return pltpu.make_async_remote_copy(src, dst, send, recv, device_id=device, device_id_type=MESH)

    def to_member(src, dst, send, recv, k):
        return remote(src, dst, send.at[k], recv.at[k], lay.member_device(g, jnp.bitwise_xor(me, k)))

    def x_copy(k):
        return to_member(x_send.at[jnp.bitwise_xor(me, k)], x_recv.at[me], xs, xr, k)

    def c_copy(k):
        return to_member(c_send.at[jnp.bitwise_xor(me, k)], c_recv.at[me], cs, cr, k)

    def gx_copy(k):
        return to_member(c_send.at[jnp.bitwise_xor(me, k)], gx_ref.at[me], gs, gr, k)

    def gate_copy(k):
        return to_member(gate_send.at[jnp.bitwise_xor(me, k)], gate_ref.at[me], ts, tr, k)

    def zy_copy(k):
        m = jnp.bitwise_xor(me, k)
        return pltpu.make_async_copy(x_send.at[m], zy_ref.at[m], zs.at[k])

    def pick_rows(m, values, target):
        slot = lax.broadcasted_iota(jnp.int32, (cap, images * height), 0) + m * cap
        hit = (code_ref[0:1, :] == slot) | (code_ref[1:2, :] == slot)
        pick = jnp.where(hit, 1.0, 0.0).astype(bf16)
        target[m] = dot(pick, values[...].reshape(images * height, width)).astype(bf16)

    def build_c(first, last):
        def build(i, carry):
            pick_rows(jnp.bitwise_xor(me, lay.nth(i + 1)), cot, c_send)
            return carry

        lax.fori_loop(first, last, build, 0)

    def weight_copies(d, first=0, count=part_rows):
        device = (lax.rem(g - d + S, S) * L + l, lax.rem(d - l + L * S, S))
        there = pl.ds(pl.multiple_of(s * part_rows + first, 16), count)
        return [
            remote(src.at[0, pl.ds(first, count)], dst.at[there], ws.at[2 * d + i], wr.at[2 * s + i], device)
            for i, (src, dst) in enumerate(((w_in_ref, w_in), (w_down_ref, w_down)))
        ]

    def weight_pieces(d, q):
        for copy in weight_copies(d, q * piece_rows, piece_rows):
            copy.start()

    def weight_local():
        mine = pl.ds(pl.multiple_of(s * part_rows, part_rows), part_rows)
        return [
            pltpu.make_async_copy(src.at[0], dst.at[mine], wr.at[2 * s + i])
            for i, (src, dst) in enumerate(((w_in_ref, w_in), (w_down_ref, w_down)))
        ]

    @pl.when(step == 0)
    def _():
        def prepare():
            first = 0
            for ref in own_refs:
                own[:, first : first + ref.shape[1]] = ref[...]
                first += ref.shape[1]
            for i in range(images):
                cot[i] = pad_rows(cot_ref[i].astype(f32), height).astype(bf16)

        greet(
            [rows.device(i, b, c, s) for _, i in rows.along_a()]
            + [rows.device(a, b2, c, s2) for _, b2, s2, _ in rows.plane()]
            + [rows.device(a, b, 1 - c, s)]
            + lay.group_peers()
            + lay.weight_peers(),
            prepare,
        )
        A, Q = rows.A, 2 * rows.S
        sl = s if rows.S > 1 else 0
        third = members // 3
        order = lay.order()
        pieces = part_rows // piece_rows
        todo = [(q, d) for q in range(pieces) for d in (*range(1, S), 0)]

        def send(first, last):
            for n in range(first, last):
                c_copy(order[n]).start()
                for q, d in todo[n * len(todo) // len(order) : (n + 1) * len(todo) // len(order)]:
                    if d:
                        weight_pieces(d, q)
                    else:

                        @pl.when(delta != 0)
                        def _():
                            weight_pieces(0, q)

        local = pltpu.make_async_copy(own, full.at[a, b, c, sl], ls.at[0])
        local.start()
        copies = [
            remote(own, full.at[a, b, c, sl], ps.at[i], pr.at[i], rows.device(a2, b, c, s))
            for i, a2 in rows.along_a()
        ]
        for copy in copies:
            copy.start()
        build_c(0, third)
        local.wait()
        for copy in copies:
            copy.wait()
        copies = [
            remote(
                full.at[:, b, c, sl], full.at[:, b, c, sl], ps.at[A + i], pr.at[A + i], rows.device(a, b2, c, s2)
            )
            for i, b2, s2, _ in rows.plane()
        ]
        for copy in copies:
            copy.start()
        build_c(third, members)
        for copy in copies:
            copy.wait()
        last = remote(
            full.at[:, :, c], full.at[:, :, c], ps.at[A + Q], pr.at[A + Q], rows.device(a, b, 1 - c, s)
        )
        last.start()

        @pl.when(delta == 0)
        def _():
            for copy in weight_local():
                copy.start()

        send(0, members - 1)
        c_recv[me] = c_send[me]
        last.wait()
        pack_ref[...] = full[...].reshape(pack_ref.shape)
        tail = pack_ref[:, 4 * width :].astype(f32).T
        gains_ref[...] = tail[GAIN_LANE : GAIN_LANE + 8, :]

    inputs = pad_rows(tok_ref[0].astype(f32), height)
    hat, _ = norm_rows(inputs)
    normed = (hat * gains_ref[0:1, :]).astype(bf16)
    qkv = dot(normed, pack_ref[:, 0 : 3 * width]).astype(bf16)
    qkv_ref[0] = qkv
    att = attend(HEADS, qkv, mask_ref[0] > 0, width, soft_ref)
    att_ref[0] = att
    residual = inputs + dot(att, pack_ref[:, 3 * width : 4 * width])
    res_ref[0] = residual
    hat, _ = norm_rows(residual)
    routed_now = (hat * gains_ref[1:2, :]).astype(bf16)
    routed_ref[0] = routed_now
    routed[step] = routed_now
    probs_ref[0] = router_softmax(dot(routed_now, pack_ref[:, 4 * width :]), experts)

    @pl.when(step == steps - 1)
    def _():
        def dispatch(i, carry):
            k = lay.nth(i)
            pick_rows(jnp.bitwise_xor(me, k), routed, x_send)
            return carry

        lax.fori_loop(1, members, dispatch, 0)
        pick_rows(me, routed, x_send)
        x_recv[me] = x_send[me]
        gwi[...] = jnp.zeros_like(gwi)
        gwd[...] = jnp.zeros_like(gwd)

        for p in range(S):
            for copy_in in range(2):
                span = pl.ds(p * part_rows, part_rows)
                dst = (w_in, w_down)[copy_in].at[span]
                src = (w_in_ref, w_down_ref)[copy_in].at[0]

                @pl.when((delta == 0) & (s == p))
                def _():
                    pltpu.make_async_copy(src, dst, wr.at[2 * p + copy_in]).wait()

                @pl.when((delta != 0) | (s != p))
                def _():
                    remote(src, dst, ws.at[0], wr.at[2 * p + copy_in], (0, 0)).wait_recv()

        for k in lay.order():
            x_copy(k).start()

        mine = lay.expert_of(g, me)
        hidden = w_in.shape[1]
        chunk = min(512, hidden)

        def work(j, carry):
            ks = (lay.nth(2 * j), lay.nth(2 * j + 1))
            ms = [jnp.bitwise_xor(me, k) for k in ks]

            @pl.when(j > 0)
            def _():
                x_copy(ks[0]).wait()
                c_copy(ks[0]).wait()

            x_copy(ks[1]).wait()
            c_copy(ks[1]).wait()
            x = jnp.concatenate([x_recv[m] for m in ms], axis=0)
            cf = jnp.concatenate([c_recv[m] for m in ms], axis=0).astype(f32)
            probs = router_softmax(dot(x, pack_ref[:, 4 * width :]), experts)
            lane = lax.broadcasted_iota(jnp.int32, probs.shape, 1)
            gate = jnp.sum(jnp.where(lane == mine, probs, 0.0), axis=1, keepdims=True)
            dy = (gate * cf).astype(bf16)
            y, gx = None, None
            for f in range(0, hidden, chunk):
                span = slice(f, f + chunk)
                value, slope = gelu_parts(dot(x, w_in[:, span]))
                act = value.astype(bf16)
                inner_grad = (dot(dy, w_down[:, span]) * slope).astype(bf16)
                y_part, gx_part = dot(act, w_down[:, span], NT), dot(inner_grad, w_in[:, span], NT)
                y = y_part if y is None else y + y_part
                gx = gx_part if gx is None else gx + gx_part
                gwd[:, span] += dot(dy, act, TN)
                gwi[:, span] += dot(x, inner_grad, TN)
            zy = (gate * y).astype(bf16)
            gxb = gx.astype(bf16)
            gate_grad = jnp.broadcast_to(jnp.sum(y * cf, axis=1, keepdims=True), (2 * cap, LANES)).T
            for q in range(2):
                c_send[ms[q]] = gxb[q * cap : (q + 1) * cap]
                x_send[ms[q]] = zy[q * cap : (q + 1) * cap]
                gate_send[ms[q]] = gate_grad[0:8, q * cap : (q + 1) * cap]

            @pl.when(j > 0)
            def _():
                gx_copy(ks[0]).start()
                gate_copy(ks[0]).start()

            gx_copy(ks[1]).start()
            gate_copy(ks[1]).start()
            zy_copy(ks[0]).start()
            zy_copy(ks[1]).start()
            return carry

        lax.fori_loop(0, members // 2, work, 0)
        keeps = [
            pltpu.make_async_copy(c_send.at[me], gx_ref.at[me], ls.at[0]),
            pltpu.make_async_copy(gate_send.at[me], gate_ref.at[me], ls.at[1]),
        ]
        for keep in keeps:
            keep.start()
        gwi_ref[...] = gwi[...].astype(bf16)
        gwd_ref[...] = gwd[...].astype(bf16)
        for keep in keeps:
            keep.wait()
        zy_copy(0).wait()
        for d in range(1, S):
            for copy in weight_copies(d):
                copy.wait_send()

        @pl.when(delta != 0)
        def _():
            for copy in weight_copies(0):
                copy.wait_send()

        def finish(k, carry):
            gx_copy(k).wait()
            gate_copy(k).wait()
            zy_copy(k).wait()
            return carry

        lax.fori_loop(1, members, finish, 0)


def front(lay, rows, experts, cap, own, tokens, mask, cotangent, codes, w_in, w_down):
    S, M = lay.S, lay.N
    images, positions, width = tokens.shape
    height = mask.shape[2]
    hidden = w_in.shape[-1]
    blocks = (M, cap, width)
    own_shape = (own[0].shape[0], sum(part.shape[1] for part in own))
    full = (rows.A, 2, 2, rows.S) + own_shape
    total = rows.A * 4 * rows.S * own_shape[0]
    dma = lambda n: pltpu.SemaphoreType.DMA((n,))
    count = rows.A + 2 * rows.S + 1
    return pl.pallas_call(
        functools.partial(front_kernel, lay, rows, experts),
        grid=(images,),
        out_shape=(
            Shape((total, own_shape[1]), bf16),
            Shape((8, width), f32),
            Shape((images, height, 3 * width), bf16),
            Shape((images, height, width), bf16),
            Shape((images, height, width), f32),
            Shape((images, HEADS, height, height), bf16),
            Shape((images, height, width), bf16),
            Shape((images, height, LANES), f32),
            Shape(blocks, bf16),
            Shape(blocks, bf16),
            Shape((M, 8, cap), f32),
            Shape((width, hidden), bf16),
            Shape((width, hidden), bf16),
        ),
        in_specs=[
            [fixed(*part.shape) for part in own],
            per_image(positions, width),
            per_image(1, height),
            fixed(*cotangent.shape),
            fixed(*codes.shape),
            anywhere(),
            anywhere(),
        ],
        out_specs=(
            fixed(total, own_shape[1]),
            fixed(8, width),
            per_image(height, 3 * width),
            per_image(height, width),
            per_image(height, width),
            per_image(HEADS, height, height),
            per_image(height, width),
            per_image(height, LANES),
            anywhere(),
            anywhere(),
            anywhere(),
            fixed(width, hidden),
            fixed(width, hidden),
        ),
        scratch_shapes=[
            pltpu.VMEM(own_shape, bf16),
            pltpu.VMEM(full, bf16),
            pltpu.VMEM((images, height, width), bf16),
            pltpu.VMEM((images, height, width), bf16),
            pltpu.VMEM((width, hidden), bf16),
            pltpu.VMEM((width, hidden), bf16),
            *[pltpu.VMEM(blocks, bf16)] * 4,
            pltpu.VMEM((M, 8, cap), f32),
            pltpu.VMEM((width, hidden), f32),
            pltpu.VMEM((width, hidden), f32),
            dma(count), dma(count), dma(2 * S), dma(2 * S),
            *[dma(M)] * 9,
            dma(2),
        ],
        compiler_params=pltpu.CompilerParams(
            collective_id=0, has_side_effects=True, vmem_limit_bytes=VMEM_LIMIT, dimension_semantics=("arbitrary",)
        ),
    )(own, tokens, mask, cotangent, codes, w_in, w_down)


def back_kernel(
    lay, rows,
    tok_ref, cot_ref, code_ref, qkv_ref, att_ref, res_ref, soft_ref, routed_ref, probs_ref,
    pack_ref, gains_ref, gx_ref, gate_ref, zy_ref, gwi_ref, gwd_ref,
    gtok_ref, mixed_ref, own_ref, gwi_parts, gwd_parts,
    gqkv, gout, grest, table, ggain, residuals, codes, zy, part, recv1, sum1, recv2, sum2, recv3,
    ps, pr, zs, zr, ws, wr, ls,
):
    step = pl.program_id(0)
    images = pl.num_programs(0)
    a, b, c, s = rows.here()
    _, _, g, l = lay.here()
    S, L = lay.S, lay.L
    me = l * S + s
    delta = lax.rem(s + l, S)
    members, _, cap = gate_ref.shape
    slots = members * cap
    height, width = att_ref.shape[1], att_ref.shape[2]
    positions = gtok_ref.shape[1]
    head = width // HEADS
    part_rows = gwi_ref.shape[0] // S
    piece_rows = max(part_rows // 8, 16)

    def remote(src, dst, send, recv, device):
        return pltpu.make_async_remote_copy(src, dst, send, recv, device_id=device, device_id_type=MESH)

    def zy_copy(k):
        m = jnp.bitwise_xor(me, k)
        return remote(zy_ref.at[m], zy.at[me], zs.at[k], zr.at[k], lay.member_device(g, m))

    owner = lax.rem(g + delta, S)

    def weight_pairs(p, first=0, count=part_rows):
        span, there = pl.ds(p * part_rows + first, count), pl.ds(first, count)
        return ((gwi_ref.at[span], gwi_parts.at[g, there]), (gwd_ref.at[span], gwd_parts.at[g, there]))

    def weight_copies(p, first=0, count=part_rows):
        return [
            remote(src, dst, ws.at[2 * p + i], wr.at[2 * g + i], (owner * L + l, p))
            for i, (src, dst) in enumerate(weight_pairs(p, first, count))
        ]

    def weight_local(p):
        return [
            pltpu.make_async_copy(src, dst, ws.at[2 * p + i]) for i, (src, dst) in enumerate(weight_pairs(p))
        ]

    def weight_pieces(p, q):
        @pl.when((delta != 0) | (s != p))
        def _():
            for copy in weight_copies(p, q * piece_rows, piece_rows):
                copy.start()

    zy_keep = pltpu.make_async_copy(zy_ref.at[me], zy.at[me], ls.at[0])

    @pl.when(step == 0)
    def _():
        def prepare():
            for ref in (gqkv, gout, grest, ggain):
                ref[...] = jnp.zeros_like(ref)
            for m in range(members):
                values = gate_ref[m].T[:, 0:1]
                high = values.astype(bf16).astype(f32)
                lane = lax.broadcasted_iota(jnp.int32, (cap, LANES), 1)
                here = lane == lay.expert_of(g, jnp.int32(m))
                span = slice(m * cap, (m + 1) * cap)
                table[span, 0:LANES] = jnp.where(here, high, 0.0).astype(bf16)
                table[span, LANES : 2 * LANES] = jnp.where(here, values - high, 0.0).astype(bf16)

        greet(
            [rows.device(i, b, c, s) for _, i in rows.along_a()]
            + [rows.device(a, b2, c, s2) for _, b2, s2, _ in rows.plane()]
            + [rows.device(a, b, 1 - c, s)]
            + lay.group_peers()
            + lay.weight_peers(),
            prepare,
        )
        zy_keep.start()
        for p in range(S):

            @pl.when((delta == 0) & (s == p))
            def _():
                for copy in weight_local(p):
                    copy.start()

    order = lay.order()
    todo = [(p, q) for q in range(part_rows // piece_rows) for p in range(S)]
    count = residuals.shape[0]
    turns = count + LATE

    def background(turn):
        for n in range(turn * len(todo) // turns, (turn + 1) * len(todo) // turns):
            weight_pieces(*todo[n])
        for k in order[2 * turn * len(order) // count : 2 * (turn + 1) * len(order) // count]:
            zy_copy(k).start()

    for turn in range(count):
        pl.when(step == turn)(functools.partial(background, turn))

    def pick_slots(code):
        slot = lax.broadcasted_iota(jnp.int32, (code.shape[0], slots), 1)
        return jnp.where((code[:, 0:1] == slot) | (code[:, 1:2] == slot), 1.0, 0.0).astype(bf16)

    wide = jnp.concatenate([code_ref[0].astype(f32), jnp.zeros((6, height), f32)], axis=0)
    codes[step] = wide.T.astype(jnp.int32)
    residuals[step] = res_ref[0]
    pick = pick_slots(codes[step])
    grad_routed = dot(pick, gx_ref[...].reshape(slots, width))
    both = dot(pick, table[...])
    grad_probs = both[:, :LANES] + both[:, LANES:]
    probs = probs_ref[0]
    grad_logits = probs * (grad_probs - jnp.sum(grad_probs * probs, axis=1, keepdims=True))
    logit_high = grad_logits.astype(bf16)
    logit_low = (grad_logits - logit_high.astype(f32)).astype(bf16)
    router = pack_ref[:, 4 * width :]
    grad_router = dot(routed_ref[0], jnp.concatenate([logit_high, logit_low], axis=1), TN)
    grest[...] += grad_router[:, :LANES] + grad_router[:, LANES:]
    grad_routed += dot(logit_high, router, NT) + dot(logit_low, router, NT)
    hat_two, inverse_two = norm_rows(res_ref[0])
    ggain[1:2, :] += jnp.sum(grad_routed * hat_two, axis=0, keepdims=True)
    grad_residual = pad_rows(cot_ref[0].astype(f32), height) + norm_back(
        grad_routed * gains_ref[1:2, :], hat_two, inverse_two
    )
    grad_att = grad_residual.astype(bf16)
    gout[...] += dot(att_ref[0], grad_att, TN)
    grad_attended = dot(grad_att, pack_ref[:, 3 * width : 4 * width], NT).astype(bf16)
    qkv, att = qkv_ref[0], att_ref[0]
    scale = head**-0.5
    grad_q, grad_k, grad_v = [], [], []
    for h in range(HEADS):
        q = qkv[:, h * head : (h + 1) * head]
        k = qkv[:, width + h * head : width + (h + 1) * head]
        v = qkv[:, 2 * width + h * head : 2 * width + (h + 1) * head]
        ga = grad_attended[:, h * head : (h + 1) * head]
        soft = soft_ref[0, h]
        grad_v.append(dot(soft, ga, TN).astype(bf16))
        row = jnp.sum(ga.astype(f32) * att[:, h * head : (h + 1) * head].astype(f32), axis=1, keepdims=True)
        grad_scores = (soft.astype(f32) * (dot(ga, v, NT) - row)).astype(bf16)
        grad_q.append((dot(grad_scores, k) * scale).astype(bf16))
        grad_k.append((dot(grad_scores, q, TN) * scale).astype(bf16))
    grad_qkv = jnp.concatenate(grad_q + grad_k + grad_v, axis=1)
    hat_one, inverse_one = norm_rows(pad_rows(tok_ref[0].astype(f32), height))
    normed = (hat_one * gains_ref[0:1, :]).astype(bf16)
    gqkv[...] += dot(normed, grad_qkv, TN)
    grad_normed = dot(grad_qkv, pack_ref[:, 0 : 3 * width], NT)
    ggain[0:1, :] += jnp.sum(grad_normed * hat_one, axis=0, keepdims=True)
    grad_inputs = grad_residual + norm_back(grad_normed * gains_ref[0:1, :], hat_one, inverse_one)
    gtok_ref[0] = grad_inputs[:positions]

    @pl.when(step == images - 1)
    def _():
        A, Q = rows.A, 2 * rows.S
        zeros = jnp.zeros((GAIN_LANE, width), f32)
        tail = jnp.concatenate([zeros, ggain[...], zeros[: GAIN_LANE - 8]], axis=0)
        grest[...] += tail.T
        shape = part.shape[:5]
        part[..., 0 : 3 * width] = gqkv[...].astype(bf16).reshape(shape + (3 * width,))
        part[..., 3 * width : 4 * width] = gout[...].astype(bf16).reshape(shape + (width,))
        part[..., 4 * width :] = grest[...].astype(bf16).reshape(shape + (LANES,))
        first = remote(part.at[:, :, 1 - c], recv1, ps.at[0], pr.at[0], rows.device(a, b, 1 - c, s))
        first.start()
        background(count)

        def wait_zy(k, carry):
            zy_copy(k).wait()
            return carry

        lax.fori_loop(1, members, wait_zy, 0)
        zy_keep.wait()

        pair = 1 if residuals.shape[0] % 8 else 2

        def mix(first_image, last_image):
            def one(i, carry):
                chosen = pl.ds(i * pair, pair)
                pick = pick_slots(codes[chosen].reshape(pair * height, 8))
                mixed = residuals[chosen].reshape(pair * height, width) + dot(pick, zy[...].reshape(slots, width))
                for n in range(pair):
                    mixed_ref[i * pair + n] = mixed[n * height : n * height + positions].astype(bf16)
                return carry

            lax.fori_loop(first_image // pair, last_image // pair, one, 0)

        mix(0, count // 4)
        first.wait()
        sum1[...] = (part[:, :, c].astype(f32) + recv1[...].astype(f32)).astype(bf16)
        copies = [
            remote(sum1.at[:, b2, sl2], recv2.at[i - 1], ps.at[i], pr.at[i], rows.device(a, b2, c, s2))
            for i, b2, s2, sl2 in rows.plane()
        ]
        for copy in copies:
            copy.start()
        background(count + 1)
        mix(count // 4, count * 3 // 4)
        for copy in copies:
            copy.wait()
        sl = s if rows.S > 1 else 0
        total = sum1[:, b, sl].astype(f32)
        for i in range(Q - 1):
            total += recv2[i].astype(f32)
        sum2[...] = total.astype(bf16)
        copies = [
            remote(sum2.at[a2], recv3.at[i - 1], ps.at[Q + i], pr.at[Q + i], rows.device(a2, b, c, s))
            for i, a2 in rows.along_a()
        ]
        for copy in copies:
            copy.start()
        for turn in range(count + 2, turns):
            background(turn)
        mix(count * 3 // 4, count)
        for copy in copies:
            copy.wait()
        final = sum2[a].astype(f32)
        for i in range(A - 1):
            final += recv3[i].astype(f32)
        own_ref[...] = final

        for p in range(S):

            @pl.when((delta == 0) & (s == p))
            def _():
                for copy in weight_local(p):
                    copy.wait()

            @pl.when((delta != 0) | (s != p))
            def _():
                for copy in weight_copies(p):
                    copy.wait_send()

        for q in range(S):
            @pl.when((delta != 0) | (g != q))
            def _():
                for i, (src, dst) in enumerate(((gwi_ref, gwi_parts), (gwd_ref, gwd_parts))):
                    span = pl.ds(0, part_rows)
                    remote(src.at[span], dst.at[q], ws.at[i], wr.at[2 * q + i], (0, 0)).wait_recv()


def back(
    lay, rows, own_height, tokens, cotangent, code, qkv, att, res, soft, routed, probs, pack, gains, gx, gate,
    zy, gwi, gwd,
):
    images, positions, width = tokens.shape
    height = att.shape[1]
    M, _, cap = gate.shape
    slots = M * cap
    A, S = rows.A, rows.S
    G = lay.S
    hidden = gwi.shape[1]
    part_rows = gwi.shape[0] // G
    columns = pack.shape[1]
    dma = lambda n: pltpu.SemaphoreType.DMA((n,))
    count = A + 2 * S + 1
    return pl.pallas_call(
        functools.partial(back_kernel, lay, rows),
        grid=(images,),
        out_shape=(
            Shape((images, positions, width), f32),
            Shape((images, positions, width), bf16),
            Shape((own_height, columns), f32),
            Shape((G, part_rows, hidden), bf16),
            Shape((G, part_rows, hidden), bf16),
        ),
        in_specs=[
            per_image(positions, width),
            per_image(positions, width),
            per_image(2, height),
            per_image(height, 3 * width),
            per_image(height, width),
            per_image(height, width),
            per_image(HEADS, height, height),
            per_image(height, width),
            per_image(height, LANES),
            fixed(*pack.shape),
            fixed(*gains.shape),
            fixed(*gx.shape),
            fixed(*gate.shape),
            anywhere(),
            anywhere(),
            anywhere(),
        ],
        out_specs=(
            per_image(positions, width),
            fixed(images, positions, width),
            fixed(own_height, columns),
            anywhere(),
            anywhere(),
        ),
        scratch_shapes=[
            pltpu.VMEM((width, 3 * width), f32),
            pltpu.VMEM((width, width), f32),
            pltpu.VMEM((width, LANES), f32),
            pltpu.VMEM((slots, 2 * LANES), bf16),
            pltpu.VMEM((8, width), f32),
            pltpu.VMEM((images, height, width), f32),
            pltpu.VMEM((images, height, 8), jnp.int32),
            pltpu.VMEM((M, cap, width), bf16),
            pltpu.VMEM((A, 2, 2, S, own_height, columns), bf16),
            pltpu.VMEM((A, 2, S, own_height, columns), bf16),
            pltpu.VMEM((A, 2, S, own_height, columns), bf16),
            pltpu.VMEM((2 * S - 1, A, own_height, columns), bf16),
            pltpu.VMEM((A, own_height, columns), bf16),
            pltpu.VMEM((A - 1, own_height, columns), bf16),
            dma(count), dma(count), dma(M), dma(M), dma(2 * G), dma(2 * G), dma(1),
        ],
        compiler_params=pltpu.CompilerParams(
            collective_id=1, has_side_effects=True, vmem_limit_bytes=VMEM_LIMIT, dimension_semantics=("arbitrary",)
        ),
    )(tokens, cotangent, code, qkv, att, res, soft, routed, probs, pack, gains, gx, gate, zy, gwi, gwd)


def finish_kernel(sums_ref, gwi_parts, gwd_parts, qkv_ref, out_ref, router_ref, gain_one, gain_two, gwi_ref, gwd_ref):
    width = out_ref.shape[1]
    step = pl.program_id(0)

    @pl.when(step == 0)
    def _():
        qkv_ref[...] = sums_ref[:, : 3 * width]
        out_ref[...] = sums_ref[:, 3 * width : 4 * width]
        rest = sums_ref[:, 4 * width :]
        router_ref[...] = rest[:, : router_ref.shape[1]]
        height = rest.shape[0]
        tall = pad_rows(rest, max(height, 8)).T
        gain_one[...] = tall[GAIN_LANE : GAIN_LANE + 1, :height]
        gain_two[...] = tall[GAIN_LANE + 1 : GAIN_LANE + 2, :height]

    for parts, ref in ((gwi_parts, gwi_ref), (gwd_parts, gwd_ref)):
        total = parts[0].astype(f32)
        for q in range(1, parts.shape[0]):
            total += parts[q].astype(f32)
        ref[0] = total


def finish(experts, width, sums, gwi, gwd):
    groups, part_rows, hidden = gwi.shape
    height = sums.shape[0]
    steps = 4 if part_rows % 64 == 0 else 1
    piece = part_rows // steps
    parts = pl.BlockSpec((groups, piece, hidden), lambda i: (0, i, 0))
    whole = pl.BlockSpec((1, piece, hidden), lambda i: (0, i, 0))
    qkv, out, router, gain_one, gain_two, gwi, gwd = pl.pallas_call(
        finish_kernel,
        grid=(steps,),
        out_shape=(
            Shape((height, 3 * width), f32),
            Shape((height, width), f32),
            Shape((height, experts), f32),
            Shape((1, height), f32),
            Shape((1, height), f32),
            Shape((1, part_rows, hidden), f32),
            Shape((1, part_rows, hidden), f32),
        ),
        in_specs=[fixed(*sums.shape), parts, parts],
        out_specs=(
            fixed(height, 3 * width),
            fixed(height, width),
            fixed(height, experts),
            fixed(1, height),
            fixed(1, height),
            whole,
            whole,
        ),
        compiler_params=pltpu.CompilerParams(vmem_limit_bytes=VMEM_LIMIT),
    )(sums, gwi, gwd)
    return qkv, out, router, gain_one.reshape(height), gain_two.reshape(height), gwi, gwd


def body(
    lay, tokens, w_qkv, w_attn_out, w_router, gain_attn, gain_moe, w_expert_in, w_expert_down, key_mask,
    expert_choice, slot_index, cotangent,
):
    images, positions, width = tokens.shape
    N, S, L = lay.N, lay.S, lay.L
    experts = w_router.shape[1]
    height = -(-positions // 16) * 16
    token_rows = images * positions
    capacity = ((token_rows * 10 + 4 * experts - 1) // (4 * experts) + 7) // 8 * 8
    dp, s, g, l = lay.here()

    lane = jnp.arange(LANES, dtype=jnp.int32)[None, :]
    rest = jnp.pad(w_router, ((0, 0), (0, LANES - experts)))
    rest = jnp.where(lane == GAIN_LANE, gain_attn[:, None], jnp.where(lane == GAIN_LANE + 1, gain_moe[:, None], rest))
    own = [w_qkv, w_attn_out, rest]
    few = w_qkv.shape[0] % 16 != 0
    if few:
        own = [lax.all_gather(part, "seq", axis=0, tiled=True) for part in own]
    rows = Rows(N, 1 if few else S)

    mask = lax.dynamic_slice_in_dim(key_mask, s * images, images, axis=0)
    mask = jnp.pad(mask, ((0, 0), (0, height - positions)))[:, None, :]
    choice, slot = expert_choice.transpose(0, 2, 1), slot_index.transpose(0, 2, 1)
    group, local = choice // L, lax.rem(choice, L)
    member = local * S + lax.rem(group - g - local + (L + 1) * S, S)
    code = jnp.where(slot >= 0, member * capacity + slot, -1)
    code = jnp.pad(code, ((0, 0), (0, 0), (0, height - positions)), constant_values=-1)
    code_rows = code.transpose(1, 0, 2).reshape(2, images * height)

    pack, gains, qkv, att, res, soft, routed, probs, gx, zy, gate, gwi, gwd = front(
        lay, rows, experts, capacity, own, tokens, mask, cotangent, code_rows, w_expert_in, w_expert_down
    )
    gtok, mixed, sums, gwi, gwd = back(
        lay, rows, own[0].shape[0], tokens, cotangent, code, qkv, att, res, soft, routed, probs, pack, gains, gx,
        gate, zy, gwi, gwd,
    )
    if few:
        sums = lax.psum_scatter(sums, "seq", scatter_dimension=0, tiled=True)
    return (mixed, gtok, *finish(experts, width, sums, gwi, gwd))


def solution(mesh):
    lay = Layout(mesh.shape["dp"], mesh.shape["seq"])
    return jax.shard_map(
        functools.partial(body, lay),
        mesh=mesh,
        in_specs=(
            P(("dp", "seq"), None, None),
            P(("dp", "seq"), None),
            P(("dp", "seq"), None),
            P(("dp", "seq"), None),
            P(("dp", "seq")),
            P(("dp", "seq")),
            P("dp", "seq", None),
            P("dp", "seq", None),
            P("dp", None),
            P(("dp", "seq"), None, None),
            P(("dp", "seq"), None, None),
            P(("dp", "seq"), None, None),
        ),
        out_specs=(
            P(("dp", "seq"), None, None),
            P(("dp", "seq"), None, None),
            P(("dp", "seq"), None),
            P(("dp", "seq"), None),
            P(("dp", "seq"), None),
            P(("dp", "seq")),
            P(("dp", "seq")),
            P("dp", "seq", None),
            P("dp", "seq", None),
        ),
        check_vma=False,
    )
```

```python
import functools

import jax
import jax.numpy as jnp
from jax import lax
from jax.experimental import pallas as pl
from jax.experimental.pallas import tpu as pltpu
from jax.sharding import PartitionSpec as P

HEADS = 8
EPSILON = 1e-06
NEGATIVE = -1e30
MESH = pl.DeviceIdType.MESH
bf16, f32 = jnp.bfloat16, jnp.float32
NN = (((1,), (0,)), ((), ()))
NT = (((1,), (1,)), ((), ()))
TN = (((0,), (0,)), ((), ()))
LANES = 128
GAIN_LANE = 64
LATE = 2
VMEM_LIMIT = 60 << 20
Shape = jax.ShapeDtypeStruct


def dot(a, b, dims=NN):
    return lax.dot_general(a, b, dims, preferred_element_type=f32)


def pad_rows(values, rows):
    extra = rows - values.shape[0]
    if extra == 0:
        return values
    return jnp.concatenate([values, jnp.zeros((extra, values.shape[1]), values.dtype)], axis=0)


def norm_rows(values):
    centred = values - jnp.mean(values, axis=-1, keepdims=True)
    inverse = lax.rsqrt(jnp.mean(centred * centred, axis=-1, keepdims=True) + EPSILON)
    return centred * inverse, inverse


def norm_back(grad_hat, normed, inverse):
    return inverse * (
        grad_hat
        - jnp.mean(grad_hat, axis=-1, keepdims=True)
        - normed * jnp.mean(grad_hat * normed, axis=-1, keepdims=True)
    )


def router_softmax(logits, experts):
    lane = lax.broadcasted_iota(jnp.int32, logits.shape, 1)
    logits = jnp.where(lane < experts, logits, NEGATIVE)
    exps = jnp.exp(logits - jnp.max(logits, axis=1, keepdims=True))
    return exps / jnp.sum(exps, axis=1, keepdims=True)


def gelu_parts(inner):
    k, c = 0.7978845608028654, 0.044715
    square = inner * inner
    t = jnp.tanh(inner * (k + (k * c) * square))
    half = 0.5 + 0.5 * t
    value = inner * half
    slope = half + value * (1.0 - half) * (2 * k + (6 * k * c) * square)
    return value, slope


def anywhere():
    return pl.BlockSpec(memory_space=pl.ANY)


def per_image(*dims):
    return pl.BlockSpec((1,) + dims, lambda i: (i,) + (0,) * len(dims))


def fixed(*dims):
    return pl.BlockSpec(dims, lambda i: (0,) * len(dims), pipeline_mode=pl.Buffered(1))


class Layout:
    def __init__(self, dp, seq):
        self.N, self.S = dp, seq
        self.L = dp // seq

    def here(self):
        dp, s = lax.axis_index("dp"), lax.axis_index("seq")
        return dp, s, dp // self.L, lax.rem(dp, self.L)

    def member_device(self, g, m):
        return (g * self.L + m // self.S, lax.rem(m, self.S))

    def group_peers(self):
        _, s, g, l = self.here()
        return [self.member_device(g, jnp.bitwise_xor(l * self.S + s, k)) for k in range(1, self.N)]

    def weight_peers(self):
        _, s, g, l = self.here()
        count = self.S * self.S
        places = [lax.rem(g * self.S + s + i, count) for i in range(1, count)]
        return [(q // self.S * self.L + l, lax.rem(q, self.S)) for q in places]

    def order(self):
        bits = [1 << i for i in range(self.N.bit_length() - 1) if 1 << i != self.S]
        left, loads, picked = list(range(1, self.N)), [0] * len(bits), []

        def after(k):
            return [load + (k & bit > 0) for load, bit in zip(loads, bits)]

        while left:
            k = min(left, key=lambda k: (max(after(k)) - min(after(k)), -sum(after(k)), k))
            left.remove(k)
            picked.append(k)
            loads = after(k)
        return picked

    def nth(self, i):
        k = jnp.int32(0)
        for n, value in enumerate(self.order()):
            k = jnp.where(i == n + 1, value, k)
        return k

    def expert_of(self, g, m):
        l, s = m // self.S, lax.rem(m, self.S)
        return lax.rem(g + s + l, self.S) * self.L + l


def greet(peers, meanwhile):
    barrier = pltpu.get_barrier_semaphore()
    for peer in peers:
        pl.semaphore_signal(barrier, inc=1, device_id=peer, device_id_type=MESH)
    meanwhile()
    pl.semaphore_wait(barrier, len(peers))


class Rows:
    def __init__(self, dp, seq):
        self.A, self.S = dp // 4, seq

    def here(self):
        dp, s = lax.axis_index("dp"), lax.axis_index("seq")
        return dp // 4, lax.rem(dp // 2, 2), lax.rem(dp, 2), s

    def device(self, a, b, c, s):
        return ((a * 2 + b) * 2 + c, s)

    def along_a(self):
        a, b, c, s = self.here()
        return [(i, lax.rem(a + i, self.A)) for i in range(1, self.A)]

    def plane(self):
        a, b, c, s = self.here()
        for i in range(1, 2 * self.S):
            if self.S == 1:
                yield i, 1 - b, s, 0
            else:
                q = lax.rem(b * self.S + s + i, 2 * self.S)
                yield i, q // self.S, lax.rem(q, self.S), lax.rem(q, self.S)


def attend(heads, qkv, keep, width, soft_ref):
    head = width // heads
    outs = []
    for h in range(heads):
        q = qkv[:, h * head : (h + 1) * head]
        k = qkv[:, width + h * head : width + (h + 1) * head]
        v = qkv[:, 2 * width + h * head : 2 * width + (h + 1) * head]
        scores = jnp.where(keep, dot(q, k, NT) * (head**-0.5), NEGATIVE)
        row_max = jnp.max(scores, axis=1, keepdims=True)
        exps = jnp.exp(scores - row_max)
        totals = jnp.sum(exps, axis=1, keepdims=True)
        soft = (exps / totals).astype(bf16)
        soft_ref[0, h] = soft
        outs.append(dot(soft, v).astype(bf16))
    return jnp.concatenate(outs, axis=1)


def front_kernel(
    lay, rows, experts,
    own_refs, tok_ref, mask_ref, cot_ref, code_ref, w_in_ref, w_down_ref,
    pack_ref, gains_ref, qkv_ref, att_ref, res_ref, soft_ref, routed_ref, probs_ref,
    gx_ref, zy_ref, gate_ref, gwi_ref, gwd_ref,
    own, full, routed, cot, w_in, w_down, x_send, c_send, x_recv, c_recv, gate_send, gwi, gwd, gwi_half, gwd_half,
    ps, pr, ws, wr, xs, xr, cs, cr, gs, gr, ts, tr, zs, ls, os,
):
    step = pl.program_id(0)
    steps = pl.num_programs(0)
    a, b, c, s = rows.here()
    _, _, g, l = lay.here()
    S, L = lay.S, lay.L
    members, cap, width = x_send.shape
    images, height = routed.shape[0], routed.shape[1]
    me = l * S + s
    delta = lax.rem(s + l, S)
    part_rows = w_in.shape[0] // S
    piece_rows = max(part_rows // 8, 16)

    def remote(src, dst, send, recv, device):
        return pltpu.make_async_remote_copy(src, dst, send, recv, device_id=device, device_id_type=MESH)

    def to_member(src, dst, send, recv, k):
        return remote(src, dst, send.at[k], recv.at[k], lay.member_device(g, jnp.bitwise_xor(me, k)))

    def x_copy(k):
        return to_member(x_send.at[jnp.bitwise_xor(me, k)], x_recv.at[me], xs, xr, k)

    def c_copy(k):
        return to_member(c_send.at[jnp.bitwise_xor(me, k)], c_recv.at[me], cs, cr, k)

    def gx_copy(k):
        return to_member(c_send.at[jnp.bitwise_xor(me, k)], gx_ref.at[me], gs, gr, k)

    def gate_copy(k):
        return to_member(gate_send.at[jnp.bitwise_xor(me, k)], gate_ref.at[me], ts, tr, k)

    def zy_copy(k):
        m = jnp.bitwise_xor(me, k)
        return pltpu.make_async_copy(x_send.at[m], zy_ref.at[m], zs.at[k])

    def pick_rows(m, values, target):
        slot = lax.broadcasted_iota(jnp.int32, (cap, images * height), 0) + m * cap
        hit = (code_ref[0:1, :] == slot) | (code_ref[1:2, :] == slot)
        pick = jnp.where(hit, 1.0, 0.0).astype(bf16)
        target[m] = dot(pick, values[...].reshape(images * height, width)).astype(bf16)

    def build_c(first, last):
        def build(i, carry):
            pick_rows(jnp.bitwise_xor(me, lay.nth(i + 1)), cot, c_send)
            return carry

        lax.fori_loop(first, last, build, 0)

    def weight_copies(d, first=0, count=part_rows):
        device = (lax.rem(g - d + S, S) * L + l, lax.rem(d - l + L * S, S))
        there = pl.ds(pl.multiple_of(s * part_rows + first, 16), count)
        return [
            remote(src.at[0, pl.ds(first, count)], dst.at[there], ws.at[2 * d + i], wr.at[2 * s + i], device)
            for i, (src, dst) in enumerate(((w_in_ref, w_in), (w_down_ref, w_down)))
        ]

    def weight_pieces(d, q):
        for copy in weight_copies(d, q * piece_rows, piece_rows):
            copy.start()

    def weight_local():
        mine = pl.ds(pl.multiple_of(s * part_rows, part_rows), part_rows)
        return [
            pltpu.make_async_copy(src.at[0], dst.at[mine], wr.at[2 * s + i])
            for i, (src, dst) in enumerate(((w_in_ref, w_in), (w_down_ref, w_down)))
        ]

    @pl.when(step == 0)
    def _():
        def prepare():
            first = 0
            for ref in own_refs:
                own[:, first : first + ref.shape[1]] = ref[...]
                first += ref.shape[1]
            for i in range(images):
                cot[i] = pad_rows(cot_ref[i].astype(f32), height).astype(bf16)

        greet(
            [rows.device(i, b, c, s) for _, i in rows.along_a()]
            + [rows.device(a, b2, c, s2) for _, b2, s2, _ in rows.plane()]
            + [rows.device(a, b, 1 - c, s)]
            + lay.group_peers()
            + lay.weight_peers(),
            prepare,
        )
        A, Q = rows.A, 2 * rows.S
        sl = s if rows.S > 1 else 0
        third = members // 3
        order = lay.order()
        pieces = part_rows // piece_rows
        todo = [(q, d) for q in range(pieces) for d in (*range(1, S), 0)]

        def send(first, last):
            for n in range(first, last):
                c_copy(order[n]).start()
                for q, d in todo[n * len(todo) // len(order) : (n + 1) * len(todo) // len(order)]:
                    if d:
                        weight_pieces(d, q)
                    else:

                        @pl.when(delta != 0)
                        def _():
                            weight_pieces(0, q)

        local = pltpu.make_async_copy(own, full.at[a, b, c, sl], ls.at[0])
        local.start()
        copies = [
            remote(own, full.at[a, b, c, sl], ps.at[i], pr.at[i], rows.device(a2, b, c, s))
            for i, a2 in rows.along_a()
        ]
        for copy in copies:
            copy.start()
        build_c(0, third)
        local.wait()
        for copy in copies:
            copy.wait()
        copies = [
            remote(
                full.at[:, b, c, sl], full.at[:, b, c, sl], ps.at[A + i], pr.at[A + i], rows.device(a, b2, c, s2)
            )
            for i, b2, s2, _ in rows.plane()
        ]
        for copy in copies:
            copy.start()
        build_c(third, members)
        for copy in copies:
            copy.wait()
        last = remote(
            full.at[:, :, c], full.at[:, :, c], ps.at[A + Q], pr.at[A + Q], rows.device(a, b, 1 - c, s)
        )
        last.start()

        @pl.when(delta == 0)
        def _():
            for copy in weight_local():
                copy.start()

        send(0, members - 1)
        c_recv[me] = c_send[me]
        last.wait()
        pack_ref[...] = full[...].reshape(pack_ref.shape)
        tail = pack_ref[:, 4 * width :].astype(f32).T
        gains_ref[...] = tail[GAIN_LANE : GAIN_LANE + 8, :]

    inputs = pad_rows(tok_ref[0].astype(f32), height)
    hat, _ = norm_rows(inputs)
    normed = (hat * gains_ref[0:1, :]).astype(bf16)
    qkv = dot(normed, pack_ref[:, 0 : 3 * width]).astype(bf16)
    qkv_ref[0] = qkv
    att = attend(HEADS, qkv, mask_ref[0] > 0, width, soft_ref)
    att_ref[0] = att
    residual = inputs + dot(att, pack_ref[:, 3 * width : 4 * width])
    res_ref[0] = residual
    hat, _ = norm_rows(residual)
    routed_now = (hat * gains_ref[1:2, :]).astype(bf16)
    routed_ref[0] = routed_now
    routed[step] = routed_now
    probs_ref[0] = router_softmax(dot(routed_now, pack_ref[:, 4 * width :]), experts)

    @pl.when(step == steps - 1)
    def _():
        def dispatch(i, carry):
            k = lay.nth(i)
            pick_rows(jnp.bitwise_xor(me, k), routed, x_send)
            return carry

        lax.fori_loop(1, members, dispatch, 0)
        pick_rows(me, routed, x_send)
        x_recv[me] = x_send[me]
        gwi[...] = jnp.zeros_like(gwi)
        gwd[...] = jnp.zeros_like(gwd)

        for p in range(S):
            for copy_in in range(2):
                span = pl.ds(p * part_rows, part_rows)
                dst = (w_in, w_down)[copy_in].at[span]
                src = (w_in_ref, w_down_ref)[copy_in].at[0]

                @pl.when((delta == 0) & (s == p))
                def _():
                    pltpu.make_async_copy(src, dst, wr.at[2 * p + copy_in]).wait()

                @pl.when((delta != 0) | (s != p))
                def _():
                    remote(src, dst, ws.at[0], wr.at[2 * p + copy_in], (0, 0)).wait_recv()

        for k in lay.order():
            x_copy(k).start()

        mine = lay.expert_of(g, me)
        hidden = w_in.shape[1]
        chunk = min(512, hidden)

        def work(j, carry):
            ks = (lay.nth(2 * j), lay.nth(2 * j + 1))
            ms = [jnp.bitwise_xor(me, k) for k in ks]

            @pl.when(j > 0)
            def _():
                x_copy(ks[0]).wait()
                c_copy(ks[0]).wait()

            x_copy(ks[1]).wait()
            c_copy(ks[1]).wait()
            x = jnp.concatenate([x_recv[m] for m in ms], axis=0)
            cf = jnp.concatenate([c_recv[m] for m in ms], axis=0).astype(f32)
            probs = router_softmax(dot(x, pack_ref[:, 4 * width :]), experts)
            lane = lax.broadcasted_iota(jnp.int32, probs.shape, 1)
            gate = jnp.sum(jnp.where(lane == mine, probs, 0.0), axis=1, keepdims=True)
            dy = (gate * cf).astype(bf16)
            y, gx = None, None
            for f in range(0, hidden, chunk):
                span = slice(f, f + chunk)
                value, slope = gelu_parts(dot(x, w_in[:, span]))
                act = value.astype(bf16)
                inner_grad = (dot(dy, w_down[:, span]) * slope).astype(bf16)
                y_part, gx_part = dot(act, w_down[:, span], NT), dot(inner_grad, w_in[:, span], NT)
                y = y_part if y is None else y + y_part
                gx = gx_part if gx is None else gx + gx_part
                gwd[:, span] += dot(dy, act, TN)
                gwi[:, span] += dot(x, inner_grad, TN)
            zy = (gate * y).astype(bf16)
            gxb = gx.astype(bf16)
            gate_grad = jnp.broadcast_to(jnp.sum(y * cf, axis=1, keepdims=True), (2 * cap, LANES)).T
            for q in range(2):
                c_send[ms[q]] = gxb[q * cap : (q + 1) * cap]
                x_send[ms[q]] = zy[q * cap : (q + 1) * cap]
                gate_send[ms[q]] = gate_grad[0:8, q * cap : (q + 1) * cap]

            @pl.when(j > 0)
            def _():
                gx_copy(ks[0]).start()
                gate_copy(ks[0]).start()

            gx_copy(ks[1]).start()
            gate_copy(ks[1]).start()
            zy_copy(ks[0]).start()
            zy_copy(ks[1]).start()
            return carry

        lax.fori_loop(0, members // 2, work, 0)
        keeps = [
            pltpu.make_async_copy(c_send.at[me], gx_ref.at[me], ls.at[0]),
            pltpu.make_async_copy(gate_send.at[me], gate_ref.at[me], ls.at[1]),
        ]
        for keep in keeps:
            keep.start()
        for i, (total, half, ref) in enumerate(((gwi, gwi_half, gwi_ref), (gwd, gwd_half, gwd_ref))):
            half[...] = total[...].astype(bf16)
            keeps.append(pltpu.make_async_copy(half, ref, os.at[i]))
            keeps[-1].start()
        zy_copy(0).wait()
        for d in range(1, S):
            for copy in weight_copies(d):
                copy.wait_send()

        @pl.when(delta != 0)
        def _():
            for copy in weight_copies(0):
                copy.wait_send()

        def finish(k, carry):
            gx_copy(k).wait()
            gate_copy(k).wait()
            zy_copy(k).wait()
            return carry

        lax.fori_loop(1, members, finish, 0)
        for keep in keeps:
            keep.wait()


def front(lay, rows, experts, cap, own, tokens, mask, cotangent, codes, w_in, w_down):
    S, M = lay.S, lay.N
    images, positions, width = tokens.shape
    height = mask.shape[2]
    hidden = w_in.shape[-1]
    blocks = (M, cap, width)
    own_shape = (own[0].shape[0], sum(part.shape[1] for part in own))
    full = (rows.A, 2, 2, rows.S) + own_shape
    total = rows.A * 4 * rows.S * own_shape[0]
    dma = lambda n: pltpu.SemaphoreType.DMA((n,))
    count = rows.A + 2 * rows.S + 1
    return pl.pallas_call(
        functools.partial(front_kernel, lay, rows, experts),
        grid=(images,),
        out_shape=(
            Shape((total, own_shape[1]), bf16),
            Shape((8, width), f32),
            Shape((images, height, 3 * width), bf16),
            Shape((images, height, width), bf16),
            Shape((images, height, width), f32),
            Shape((images, HEADS, height, height), bf16),
            Shape((images, height, width), bf16),
            Shape((images, height, LANES), f32),
            Shape(blocks, bf16),
            Shape(blocks, bf16),
            Shape((M, 8, cap), f32),
            Shape((width, hidden), bf16),
            Shape((width, hidden), bf16),
        ),
        in_specs=[
            [fixed(*part.shape) for part in own],
            per_image(positions, width),
            per_image(1, height),
            fixed(*cotangent.shape),
            fixed(*codes.shape),
            anywhere(),
            anywhere(),
        ],
        out_specs=(
            fixed(total, own_shape[1]),
            fixed(8, width),
            per_image(height, 3 * width),
            per_image(height, width),
            per_image(height, width),
            per_image(HEADS, height, height),
            per_image(height, width),
            per_image(height, LANES),
            anywhere(),
            anywhere(),
            anywhere(),
            anywhere(),
            anywhere(),
        ),
        scratch_shapes=[
            pltpu.VMEM(own_shape, bf16),
            pltpu.VMEM(full, bf16),
            pltpu.VMEM((images, height, width), bf16),
            pltpu.VMEM((images, height, width), bf16),
            pltpu.VMEM((width, hidden), bf16),
            pltpu.VMEM((width, hidden), bf16),
            *[pltpu.VMEM(blocks, bf16)] * 4,
            pltpu.VMEM((M, 8, cap), f32),
            pltpu.VMEM((width, hidden), f32),
            pltpu.VMEM((width, hidden), f32),
            pltpu.VMEM((width, hidden), bf16),
            pltpu.VMEM((width, hidden), bf16),
            dma(count), dma(count), dma(2 * S), dma(2 * S),
            *[dma(M)] * 9,
            dma(2),
            dma(2),
        ],
        compiler_params=pltpu.CompilerParams(
            collective_id=0, has_side_effects=True, vmem_limit_bytes=VMEM_LIMIT, dimension_semantics=("arbitrary",)
        ),
    )(own, tokens, mask, cotangent, codes, w_in, w_down)


def back_kernel(
    lay, rows,
    tok_ref, cot_ref, code_ref, qkv_ref, att_ref, res_ref, soft_ref, routed_ref, probs_ref,
    pack_ref, gains_ref, gx_ref, gate_ref, zy_ref, gwi_ref, gwd_ref,
    gtok_ref, mixed_ref, own_ref, gwi_parts, gwd_parts,
    gqkv, gout, grest, table, ggain, residuals, codes, zy, part, recv1, sum1, recv2, sum2, recv3,
    ps, pr, zs, zr, ws, wr, ls,
):
    step = pl.program_id(0)
    images = pl.num_programs(0)
    a, b, c, s = rows.here()
    _, _, g, l = lay.here()
    S, L = lay.S, lay.L
    me = l * S + s
    delta = lax.rem(s + l, S)
    members, _, cap = gate_ref.shape
    slots = members * cap
    height, width = att_ref.shape[1], att_ref.shape[2]
    positions = gtok_ref.shape[1]
    head = width // HEADS
    part_rows = gwi_ref.shape[0] // S
    piece_rows = max(part_rows // 8, 16)

    def remote(src, dst, send, recv, device):
        return pltpu.make_async_remote_copy(src, dst, send, recv, device_id=device, device_id_type=MESH)

    def zy_copy(k):
        m = jnp.bitwise_xor(me, k)
        return remote(zy_ref.at[m], zy.at[me], zs.at[k], zr.at[k], lay.member_device(g, m))

    owner = lax.rem(g + delta, S)

    def weight_pairs(p, first=0, count=part_rows):
        span, there = pl.ds(p * part_rows + first, count), pl.ds(first, count)
        return ((gwi_ref.at[span], gwi_parts.at[g, there]), (gwd_ref.at[span], gwd_parts.at[g, there]))

    def weight_copies(p, first=0, count=part_rows):
        return [
            remote(src, dst, ws.at[2 * p + i], wr.at[2 * g + i], (owner * L + l, p))
            for i, (src, dst) in enumerate(weight_pairs(p, first, count))
        ]

    def weight_local(p):
        return [
            pltpu.make_async_copy(src, dst, ws.at[2 * p + i]) for i, (src, dst) in enumerate(weight_pairs(p))
        ]

    def weight_pieces(p, q):
        @pl.when((delta != 0) | (s != p))
        def _():
            for copy in weight_copies(p, q * piece_rows, piece_rows):
                copy.start()

    zy_keep = pltpu.make_async_copy(zy_ref.at[me], zy.at[me], ls.at[0])

    @pl.when(step == 0)
    def _():
        def prepare():
            for ref in (gqkv, gout, grest, ggain):
                ref[...] = jnp.zeros_like(ref)
            for m in range(members):
                values = gate_ref[m].T[:, 0:1]
                high = values.astype(bf16).astype(f32)
                lane = lax.broadcasted_iota(jnp.int32, (cap, LANES), 1)
                here = lane == lay.expert_of(g, jnp.int32(m))
                span = slice(m * cap, (m + 1) * cap)
                table[span, 0:LANES] = jnp.where(here, high, 0.0).astype(bf16)
                table[span, LANES : 2 * LANES] = jnp.where(here, values - high, 0.0).astype(bf16)

        greet(
            [rows.device(i, b, c, s) for _, i in rows.along_a()]
            + [rows.device(a, b2, c, s2) for _, b2, s2, _ in rows.plane()]
            + [rows.device(a, b, 1 - c, s)]
            + lay.group_peers()
            + lay.weight_peers(),
            prepare,
        )
        zy_keep.start()
        for p in range(S):

            @pl.when((delta == 0) & (s == p))
            def _():
                for copy in weight_local(p):
                    copy.start()

    order = lay.order()
    todo = [(p, q) for q in range(part_rows // piece_rows) for p in range(S)]
    count = residuals.shape[0]
    turns = count + LATE

    def background(turn):
        for n in range(turn * len(todo) // turns, (turn + 1) * len(todo) // turns):
            weight_pieces(*todo[n])
        for k in order[2 * turn * len(order) // count : 2 * (turn + 1) * len(order) // count]:
            zy_copy(k).start()

    for turn in range(count):
        pl.when(step == turn)(functools.partial(background, turn))

    def pick_slots(code):
        slot = lax.broadcasted_iota(jnp.int32, (code.shape[0], slots), 1)
        return jnp.where((code[:, 0:1] == slot) | (code[:, 1:2] == slot), 1.0, 0.0).astype(bf16)

    wide = jnp.concatenate([code_ref[0].astype(f32), jnp.zeros((6, height), f32)], axis=0)
    codes[step] = wide.T.astype(jnp.int32)
    residuals[step] = res_ref[0]
    pick = pick_slots(codes[step])
    grad_routed = dot(pick, gx_ref[...].reshape(slots, width))
    both = dot(pick, table[...])
    grad_probs = both[:, :LANES] + both[:, LANES:]
    probs = probs_ref[0]
    grad_logits = probs * (grad_probs - jnp.sum(grad_probs * probs, axis=1, keepdims=True))
    logit_high = grad_logits.astype(bf16)
    logit_low = (grad_logits - logit_high.astype(f32)).astype(bf16)
    router = pack_ref[:, 4 * width :]
    grad_router = dot(routed_ref[0], jnp.concatenate([logit_high, logit_low], axis=1), TN)
    grest[...] += grad_router[:, :LANES] + grad_router[:, LANES:]
    grad_routed += dot(logit_high, router, NT) + dot(logit_low, router, NT)
    hat_two, inverse_two = norm_rows(res_ref[0])
    ggain[1:2, :] += jnp.sum(grad_routed * hat_two, axis=0, keepdims=True)
    grad_residual = pad_rows(cot_ref[0].astype(f32), height) + norm_back(
        grad_routed * gains_ref[1:2, :], hat_two, inverse_two
    )
    grad_att = grad_residual.astype(bf16)
    gout[...] += dot(att_ref[0], grad_att, TN)
    grad_attended = dot(grad_att, pack_ref[:, 3 * width : 4 * width], NT).astype(bf16)
    qkv, att = qkv_ref[0], att_ref[0]
    scale = head**-0.5
    grad_q, grad_k, grad_v = [], [], []
    for h in range(HEADS):
        q = qkv[:, h * head : (h + 1) * head]
        k = qkv[:, width + h * head : width + (h + 1) * head]
        v = qkv[:, 2 * width + h * head : 2 * width + (h + 1) * head]
        ga = grad_attended[:, h * head : (h + 1) * head]
        soft = soft_ref[0, h]
        grad_v.append(dot(soft, ga, TN).astype(bf16))
        row = jnp.sum(ga.astype(f32) * att[:, h * head : (h + 1) * head].astype(f32), axis=1, keepdims=True)
        grad_scores = (soft.astype(f32) * (dot(ga, v, NT) - row)).astype(bf16)
        grad_q.append((dot(grad_scores, k) * scale).astype(bf16))
        grad_k.append((dot(grad_scores, q, TN) * scale).astype(bf16))
    grad_qkv = jnp.concatenate(grad_q + grad_k + grad_v, axis=1)
    hat_one, inverse_one = norm_rows(pad_rows(tok_ref[0].astype(f32), height))
    normed = (hat_one * gains_ref[0:1, :]).astype(bf16)
    gqkv[...] += dot(normed, grad_qkv, TN)
    grad_normed = dot(grad_qkv, pack_ref[:, 0 : 3 * width], NT)
    ggain[0:1, :] += jnp.sum(grad_normed * hat_one, axis=0, keepdims=True)
    grad_inputs = grad_residual + norm_back(grad_normed * gains_ref[0:1, :], hat_one, inverse_one)
    gtok_ref[0] = grad_inputs[:positions]

    @pl.when(step == images - 1)
    def _():
        A, Q = rows.A, 2 * rows.S
        zeros = jnp.zeros((GAIN_LANE, width), f32)
        tail = jnp.concatenate([zeros, ggain[...], zeros[: GAIN_LANE - 8]], axis=0)
        grest[...] += tail.T
        shape = part.shape[:5]
        part[..., 0 : 3 * width] = gqkv[...].astype(bf16).reshape(shape + (3 * width,))
        part[..., 3 * width : 4 * width] = gout[...].astype(bf16).reshape(shape + (width,))
        part[..., 4 * width :] = grest[...].astype(bf16).reshape(shape + (LANES,))
        first = remote(part.at[:, :, 1 - c], recv1, ps.at[0], pr.at[0], rows.device(a, b, 1 - c, s))
        first.start()
        background(count)

        def wait_zy(k, carry):
            zy_copy(k).wait()
            return carry

        lax.fori_loop(1, members, wait_zy, 0)
        zy_keep.wait()

        pair = 1 if residuals.shape[0] % 8 else 2

        def mix(first_image, last_image):
            def one(i, carry):
                chosen = pl.ds(i * pair, pair)
                pick = pick_slots(codes[chosen].reshape(pair * height, 8))
                mixed = residuals[chosen].reshape(pair * height, width) + dot(pick, zy[...].reshape(slots, width))
                for n in range(pair):
                    mixed_ref[i * pair + n] = mixed[n * height : n * height + positions].astype(bf16)
                return carry

            lax.fori_loop(first_image // pair, last_image // pair, one, 0)

        mix(0, count // 4)
        first.wait()
        sum1[...] = (part[:, :, c].astype(f32) + recv1[...].astype(f32)).astype(bf16)
        copies = [
            remote(sum1.at[:, b2, sl2], recv2.at[i - 1], ps.at[i], pr.at[i], rows.device(a, b2, c, s2))
            for i, b2, s2, sl2 in rows.plane()
        ]
        for copy in copies:
            copy.start()
        background(count + 1)
        mix(count // 4, count * 3 // 4)
        for copy in copies:
            copy.wait()
        sl = s if rows.S > 1 else 0
        total = sum1[:, b, sl].astype(f32)
        for i in range(Q - 1):
            total += recv2[i].astype(f32)
        sum2[...] = total.astype(bf16)
        copies = [
            remote(sum2.at[a2], recv3.at[i - 1], ps.at[Q + i], pr.at[Q + i], rows.device(a2, b, c, s))
            for i, a2 in rows.along_a()
        ]
        for copy in copies:
            copy.start()
        for turn in range(count + 2, turns):
            background(turn)
        mix(count * 3 // 4, count)
        for copy in copies:
            copy.wait()
        final = sum2[a].astype(f32)
        for i in range(A - 1):
            final += recv3[i].astype(f32)
        own_ref[...] = final

        for p in range(S):

            @pl.when((delta == 0) & (s == p))
            def _():
                for copy in weight_local(p):
                    copy.wait()

            @pl.when((delta != 0) | (s != p))
            def _():
                for copy in weight_copies(p):
                    copy.wait_send()

        for q in range(S):
            @pl.when((delta != 0) | (g != q))
            def _():
                for i, (src, dst) in enumerate(((gwi_ref, gwi_parts), (gwd_ref, gwd_parts))):
                    span = pl.ds(0, part_rows)
                    remote(src.at[span], dst.at[q], ws.at[i], wr.at[2 * q + i], (0, 0)).wait_recv()


def back(
    lay, rows, own_height, tokens, cotangent, code, qkv, att, res, soft, routed, probs, pack, gains, gx, gate,
    zy, gwi, gwd,
):
    images, positions, width = tokens.shape
    height = att.shape[1]
    M, _, cap = gate.shape
    slots = M * cap
    A, S = rows.A, rows.S
    G = lay.S
    hidden = gwi.shape[1]
    part_rows = gwi.shape[0] // G
    columns = pack.shape[1]
    dma = lambda n: pltpu.SemaphoreType.DMA((n,))
    count = A + 2 * S + 1
    return pl.pallas_call(
        functools.partial(back_kernel, lay, rows),
        grid=(images,),
        out_shape=(
            Shape((images, positions, width), f32),
            Shape((images, positions, width), bf16),
            Shape((own_height, columns), f32),
            Shape((G, part_rows, hidden), bf16),
            Shape((G, part_rows, hidden), bf16),
        ),
        in_specs=[
            per_image(positions, width),
            per_image(positions, width),
            per_image(2, height),
            per_image(height, 3 * width),
            per_image(height, width),
            per_image(height, width),
            per_image(HEADS, height, height),
            per_image(height, width),
            per_image(height, LANES),
            fixed(*pack.shape),
            fixed(*gains.shape),
            fixed(*gx.shape),
            fixed(*gate.shape),
            anywhere(),
            anywhere(),
            anywhere(),
        ],
        out_specs=(
            per_image(positions, width),
            fixed(images, positions, width),
            fixed(own_height, columns),
            anywhere(),
            anywhere(),
        ),
        scratch_shapes=[
            pltpu.VMEM((width, 3 * width), f32),
            pltpu.VMEM((width, width), f32),
            pltpu.VMEM((width, LANES), f32),
            pltpu.VMEM((slots, 2 * LANES), bf16),
            pltpu.VMEM((8, width), f32),
            pltpu.VMEM((images, height, width), f32),
            pltpu.VMEM((images, height, 8), jnp.int32),
            pltpu.VMEM((M, cap, width), bf16),
            pltpu.VMEM((A, 2, 2, S, own_height, columns), bf16),
            pltpu.VMEM((A, 2, S, own_height, columns), bf16),
            pltpu.VMEM((A, 2, S, own_height, columns), bf16),
            pltpu.VMEM((2 * S - 1, A, own_height, columns), bf16),
            pltpu.VMEM((A, own_height, columns), bf16),
            pltpu.VMEM((A - 1, own_height, columns), bf16),
            dma(count), dma(count), dma(M), dma(M), dma(2 * G), dma(2 * G), dma(1),
        ],
        compiler_params=pltpu.CompilerParams(
            collective_id=1, has_side_effects=True, vmem_limit_bytes=VMEM_LIMIT, dimension_semantics=("arbitrary",)
        ),
    )(tokens, cotangent, code, qkv, att, res, soft, routed, probs, pack, gains, gx, gate, zy, gwi, gwd)


def finish_kernel(sums_ref, gwi_parts, gwd_parts, qkv_ref, out_ref, router_ref, gain_one, gain_two, gwi_ref, gwd_ref):
    width = out_ref.shape[1]
    step = pl.program_id(0)

    @pl.when(step == 0)
    def _():
        qkv_ref[...] = sums_ref[:, : 3 * width]
        out_ref[...] = sums_ref[:, 3 * width : 4 * width]
        rest = sums_ref[:, 4 * width :]
        router_ref[...] = rest[:, : router_ref.shape[1]]
        height = rest.shape[0]
        tall = pad_rows(rest, max(height, 8)).T
        gain_one[...] = tall[GAIN_LANE : GAIN_LANE + 1, :height]
        gain_two[...] = tall[GAIN_LANE + 1 : GAIN_LANE + 2, :height]

    for parts, ref in ((gwi_parts, gwi_ref), (gwd_parts, gwd_ref)):
        total = parts[0].astype(f32)
        for q in range(1, parts.shape[0]):
            total += parts[q].astype(f32)
        ref[0] = total


def finish(experts, width, sums, gwi, gwd):
    groups, part_rows, hidden = gwi.shape
    height = sums.shape[0]
    steps = 4 if part_rows % 64 == 0 else 1
    piece = part_rows // steps
    parts = pl.BlockSpec((groups, piece, hidden), lambda i: (0, i, 0))
    whole = pl.BlockSpec((1, piece, hidden), lambda i: (0, i, 0))
    qkv, out, router, gain_one, gain_two, gwi, gwd = pl.pallas_call(
        finish_kernel,
        grid=(steps,),
        out_shape=(
            Shape((height, 3 * width), f32),
            Shape((height, width), f32),
            Shape((height, experts), f32),
            Shape((1, height), f32),
            Shape((1, height), f32),
            Shape((1, part_rows, hidden), f32),
            Shape((1, part_rows, hidden), f32),
        ),
        in_specs=[fixed(*sums.shape), parts, parts],
        out_specs=(
            fixed(height, 3 * width),
            fixed(height, width),
            fixed(height, experts),
            fixed(1, height),
            fixed(1, height),
            whole,
            whole,
        ),
        compiler_params=pltpu.CompilerParams(vmem_limit_bytes=VMEM_LIMIT),
    )(sums, gwi, gwd)
    return qkv, out, router, gain_one.reshape(height), gain_two.reshape(height), gwi, gwd


def body(
    lay, tokens, w_qkv, w_attn_out, w_router, gain_attn, gain_moe, w_expert_in, w_expert_down, key_mask,
    expert_choice, slot_index, cotangent,
):
    images, positions, width = tokens.shape
    N, S, L = lay.N, lay.S, lay.L
    experts = w_router.shape[1]
    height = -(-positions // 16) * 16
    token_rows = images * positions
    capacity = ((token_rows * 10 + 4 * experts - 1) // (4 * experts) + 7) // 8 * 8
    dp, s, g, l = lay.here()

    lane = jnp.arange(LANES, dtype=jnp.int32)[None, :]
    rest = jnp.pad(w_router, ((0, 0), (0, LANES - experts)))
    rest = jnp.where(lane == GAIN_LANE, gain_attn[:, None], jnp.where(lane == GAIN_LANE + 1, gain_moe[:, None], rest))
    own = [w_qkv, w_attn_out, rest]
    few = w_qkv.shape[0] % 16 != 0
    if few:
        own = [lax.all_gather(part, "seq", axis=0, tiled=True) for part in own]
    rows = Rows(N, 1 if few else S)

    mask = lax.dynamic_slice_in_dim(key_mask, s * images, images, axis=0)
    mask = jnp.pad(mask, ((0, 0), (0, height - positions)))[:, None, :]
    choice, slot = expert_choice.transpose(0, 2, 1), slot_index.transpose(0, 2, 1)
    group, local = choice // L, lax.rem(choice, L)
    member = local * S + lax.rem(group - g - local + (L + 1) * S, S)
    code = jnp.where(slot >= 0, member * capacity + slot, -1)
    code = jnp.pad(code, ((0, 0), (0, 0), (0, height - positions)), constant_values=-1)
    code_rows = code.transpose(1, 0, 2).reshape(2, images * height)

    pack, gains, qkv, att, res, soft, routed, probs, gx, zy, gate, gwi, gwd = front(
        lay, rows, experts, capacity, own, tokens, mask, cotangent, code_rows, w_expert_in, w_expert_down
    )
    gtok, mixed, sums, gwi, gwd = back(
        lay, rows, own[0].shape[0], tokens, cotangent, code, qkv, att, res, soft, routed, probs, pack, gains, gx,
        gate, zy, gwi, gwd,
    )
    if few:
        sums = lax.psum_scatter(sums, "seq", scatter_dimension=0, tiled=True)
    return (mixed, gtok, *finish(experts, width, sums, gwi, gwd))


def solution(mesh):
    lay = Layout(mesh.shape["dp"], mesh.shape["seq"])
    return jax.shard_map(
        functools.partial(body, lay),
        mesh=mesh,
        in_specs=(
            P(("dp", "seq"), None, None),
            P(("dp", "seq"), None),
            P(("dp", "seq"), None),
            P(("dp", "seq"), None),
            P(("dp", "seq")),
            P(("dp", "seq")),
            P("dp", "seq", None),
            P("dp", "seq", None),
            P("dp", None),
            P(("dp", "seq"), None, None),
            P(("dp", "seq"), None, None),
            P(("dp", "seq"), None, None),
        ),
        out_specs=(
            P(("dp", "seq"), None, None),
            P(("dp", "seq"), None, None),
            P(("dp", "seq"), None),
            P(("dp", "seq"), None),
            P(("dp", "seq"), None),
            P(("dp", "seq")),
            P(("dp", "seq")),
            P("dp", "seq", None),
            P("dp", "seq", None),
        ),
        check_vma=False,
    )
```
